1024 devices in a mesh: node: 32 (over z, core), local: 32 (over x, y).
Axes of the slice: x: 4, y: 8, z: 16, core: 2. Of those that a mesh axis runs over, the one named last changes fastest.
Arguments:
- tokens: bfloat16 [3072, 2048], P('node', 'local'), may hold values from -6 to 6
- grad_out: bfloat16 [3072, 2048], P('node', 'local'), may hold values from -1.1953125 to 1.1953125
- probs: bfloat16 [3072, 8], P('node'), may hold values from 0.019897461 to 0.5
- slot_of: int32 [3072, 8], P('node'), may hold values from 0 to 255, all different within a row; in each aligned block of 96 rows (0 to 95, 96 to 191, ...) at most 6 rows name the same one
- w_gate: bfloat16 [1024, 2048, 192], P(('node', 'local')), may hold values from -0.125 to 0.125
- w_up: bfloat16 [1024, 2048, 192], P(('node', 'local')), may hold values from -0.125 to 0.125
- w_down: bfloat16 [1024, 192, 2048], P(('node', 'local')), may hold values from -0.21875 to 0.21875
Outputs:
- d_tokens: bfloat16 [3072, 2048], P('node', 'local')
- d_probs: float32 [3072, 8], P('node')
- grad_gate: bfloat16 [1024, 2048, 192], P(('node', 'local'))
The draws below stay inside these ranges and needn't reach their ends.
Inputs may be any that keep to these rules, and one draw needn't show every extreme that they name: `slot_of`: each token names 8 different slots. Among the 96 tokens of one index of node (aligned blocks of rows), no slot is named by more than 6 tokens, and in some block some slot is named by exactly 6.
All inputs are finite; a program needn't handle non-finite values.
Results may differ from the reference program's by a relative error of at most 0.0057.
Values may be sent and summed in bfloat16 or wider, within the bound.
A program may use at most 32 MiB of HBM per device.

```python
import math
import jax
import jax.numpy as jnp
import numpy as np
from jax import lax

D = 2048
FF = 768
TOPK = 8
TOK_NODE = 96
TOKENS = 3072
SLOTS = 256
CAP = 6
N_NODE = 32


def block_levels(own_key, extent, pieces, least, high):
    factor_of = 1.0
    for dim, blocks in pieces:
        draws = jax.random.uniform(jax.random.fold_in(jax.random.fold_in(own_key, 6), dim), (blocks,), jnp.float32, least / len(pieces), high / len(pieces))
        factor_of = factor_of * jnp.repeat(jnp.exp(draws), extent[dim] // blocks).reshape((-1,) + (1,) * (len(extent) - 1 - dim))
    return factor_of


def deal_out(own_key, own, number, rows, count, top, limit, skew):
    sequence = jax.random.permutation(own_key, count)
    crowded, usual = portions_of(count, rows * top, limit, skew, True), portions_of(count, rows * top, limit, skew, False)
    places = jnp.arange(count)

    def named(tallies, offset_by):
        used = int((tallies > 0).sum())
        fixed = max(1, used // 4)
        shifted = fixed + (places - fixed + offset_by * (used - fixed)) % max(1, count - fixed)
        return jnp.zeros((count,), jnp.int32).at[sequence[jnp.where(places < fixed, places, shifted)]].set(jnp.asarray(tallies, jnp.int32))

    tallies = jnp.where(number % 4 == 0, named(crowded, number // 4), named(usual, number - number // 4 - 1))
    mixed = jax.random.permutation(jax.random.fold_in(own, 3), count)
    giver, receiver = mixed[0:count // 2 * 2:2], mixed[1:count // 2 * 2:2]
    room = jnp.minimum(tallies[giver] - 1, limit - tallies[receiver]) // 2
    room = jnp.where((giver == sequence[0]) | (receiver == sequence[0]) | (tallies[receiver] == 0), 0, jnp.maximum(room, 0))
    shifted = jax.random.randint(jax.random.fold_in(own, 4), (count // 2,), 0, 1 << 20) % (room + 1)
    tallies = tallies.at[giver].add(-shifted).at[receiver].add(shifted)
    members = jnp.searchsorted(jnp.cumsum(tallies), jnp.arange(rows * top), side="right").astype(jnp.int32)
    grid = members.reshape(top, rows).T
    grid = grid[jax.random.permutation(jax.random.fold_in(own, 1), rows)]
    offset_by = jax.random.randint(jax.random.fold_in(own, 2), (rows, 1), 0, top)
    return jnp.take_along_axis(grid, (jnp.arange(top)[None, :] + offset_by) % top, axis=1)


def portions_of(number_of, total, reach, slope, full):
    weights = [(1 << 20) // math.isqrt(rank ** slope) + 1 for rank in range(1, number_of + 1)]
    largest = reach if full else min(reach, max(-(-total // number_of), total * weights[0] // sum(weights)))
    least = 1 if total - largest >= number_of - 1 else 0
    holding, spare = [largest] + [least] * (number_of - 1), total - largest - least * (number_of - 1)
    while spare > 0:
        candidates = [i for i in range(1, number_of) if holding[i] < largest] or [i for i in range(1, number_of) if holding[i] < reach]
        whole, remaining = sum([weights[i] for i in candidates]), spare
        for i in candidates:
            more = min(reach - holding[i], max(1, remaining * weights[i] // whole), spare)
            holding[i] = holding[i] + more
            spare = spare - more
    return np.array(holding)


def scatter_about(own_key, shape, deviation, most, cuts=(), held_as=jnp.bfloat16):
    gain = block_levels(own_key, shape, cuts, -0.22, 0.18) if cuts else 1.0
    entries = jax.random.normal(own_key, shape, jnp.float32) * deviation * gain
    return jnp.minimum(jnp.maximum(entries, -most), most).astype(held_as)


def setup_inputs(seed: int = 0) -> dict:
    splits = jax.random.split(jax.random.key(seed), 8)
    tokens = scatter_about(splits[0], (TOKENS, D), 1.0, 6.0, ((0, 32), (1, 32)))
    grad_out = scatter_about(splits[1], (TOKENS, D), 0.2, 1.1953125, ((0, 32), (1, 32)))
    probs = jnp.clip(jnp.exp(math.log(0.5) - 3.224016 * jax.random.uniform(splits[2], (TOKENS, TOPK), jnp.float32) ** block_levels(splits[2], (TOKENS, TOPK), ((0, 32),), -0.2, 0.2)), 0.019897461, 0.5).astype(jnp.bfloat16)
    slot_of_keys = jax.random.split(jax.random.fold_in(splits[3], 1), TOKENS // TOK_NODE)
    slot_of_turns = jax.random.permutation(jax.random.fold_in(splits[3], 3), TOKENS // TOK_NODE)
    slot_of = jax.vmap(lambda own, number: deal_out(jax.random.fold_in(splits[3], 2), own, number, TOK_NODE, SLOTS, TOPK, CAP, 2))(slot_of_keys, slot_of_turns).reshape((TOKENS, TOPK))
    w_gate = scatter_about(splits[4], (SLOTS * 4, D, FF // 4), D ** -0.5, 0.125, ((0, 1024),))
    w_up = scatter_about(splits[5], (SLOTS * 4, D, FF // 4), D ** -0.5, 0.125, ((0, 1024),))
    w_down = scatter_about(splits[6], (SLOTS * 4, FF // 4, D), FF ** -0.5, 0.21875, ((0, 1024),))
    return dict(tokens=tokens, grad_out=grad_out, probs=probs, slot_of=slot_of, w_gate=w_gate, w_up=w_up, w_down=w_down)


def gated_parts(gate):
    sigmoid_gate = jax.nn.sigmoid(gate)
    return gate * sigmoid_gate, sigmoid_gate * (1.0 + gate * (1.0 - sigmoid_gate))


def pair_ranks(slot_row, slot_count):
    onehot = (slot_row[:, None] == jnp.arange(slot_count, dtype=jnp.int32)[None, :]).astype(jnp.int32)
    return jnp.sum((jnp.cumsum(onehot, axis=0) - onehot) * onehot, axis=1).astype(jnp.int32)


def reference(tokens, grad_out, probs, slot_of, w_gate, w_up, w_down):
    token_count, width = tokens.shape
    top_count = slot_of.shape[1]
    quarter = w_gate.shape[2]
    slot_count = w_gate.shape[0] // 4
    per_slot = N_NODE * CAP
    pair_total = token_count * top_count
    node_pairs = slot_of.reshape(N_NODE, TOK_NODE * top_count)
    ranks = lax.map(lambda row: pair_ranks(row, slot_count), node_pairs)
    node_index = jnp.arange(N_NODE, dtype=jnp.int32)[:, None]
    row_place = (node_pairs * per_slot + node_index * CAP + ranks).reshape(pair_total)
    pair_ids = jnp.arange(pair_total, dtype=jnp.int32)
    table = jnp.full((slot_count * per_slot,), pair_total, jnp.int32).at[row_place].set(pair_ids)
    table = table.reshape(slot_count, per_slot)
    flat_probs = probs.reshape(pair_total)

    def one_slot(carry, slot_index):
        token_grad, prob_grad = carry
        owners = table[slot_index]
        valid = owners < pair_total
        safe = jnp.minimum(owners, pair_total - 1)
        token_index = (safe // top_count).astype(jnp.int32)
        input_rows = jnp.where(valid[:, None], tokens[token_index], jnp.zeros((), tokens.dtype))
        grad_rows = jnp.where(valid[:, None], grad_out[token_index], jnp.zeros((), grad_out.dtype))
        weight_rows = jnp.where(valid, flat_probs[safe].astype(jnp.float32), jnp.zeros((), jnp.float32))
        start = (slot_index * 4).astype(jnp.int32)
        gate_full = jnp.transpose(lax.dynamic_slice_in_dim(w_gate, start, 4, 0), (1, 0, 2)).reshape(width, 4 * quarter)
        up_full = jnp.transpose(lax.dynamic_slice_in_dim(w_up, start, 4, 0), (1, 0, 2)).reshape(width, 4 * quarter)
        down_full = lax.dynamic_slice_in_dim(w_down, start, 4, 0).reshape(4 * quarter, width)
        gate = jnp.dot(input_rows, gate_full, preferred_element_type=jnp.float32)
        up_proj = jnp.dot(input_rows, up_full, preferred_element_type=jnp.float32)
        silu_gate, silu_slope = gated_parts(gate)
        hidden = (silu_gate * up_proj).astype(jnp.bfloat16)
        out_full = jnp.dot(hidden, down_full, preferred_element_type=jnp.float32)
        prob_terms = jnp.sum(grad_rows.astype(jnp.float32) * out_full, axis=1)
        d_out = (weight_rows[:, None] * grad_rows.astype(jnp.float32)).astype(jnp.bfloat16)
        d_hidden = jnp.dot(d_out, down_full.T, preferred_element_type=jnp.float32)
        d_gate = (d_hidden * up_proj * silu_slope).astype(jnp.bfloat16)
        d_up = (d_hidden * silu_gate).astype(jnp.bfloat16)
        d_pair = jnp.dot(d_gate, gate_full.T, preferred_element_type=jnp.float32) + jnp.dot(d_up, up_full.T, preferred_element_type=jnp.float32)
        target = jnp.where(valid, token_index, token_count).astype(jnp.int32)
        token_grad = token_grad.at[target].add(d_pair, mode="drop")
        pair_target = jnp.where(valid, owners, pair_total).astype(jnp.int32)
        prob_grad = prob_grad.at[pair_target].set(prob_terms, mode="drop")
        gate_grad = jnp.dot(input_rows.T, d_gate, preferred_element_type=jnp.float32).astype(jnp.bfloat16)
        gate_grad = jnp.transpose(gate_grad.reshape(width, 4, quarter), (1, 0, 2))
        return (token_grad, prob_grad), gate_grad

    start_carry = (jnp.zeros((token_count, width), jnp.float32), jnp.zeros((pair_total,), jnp.float32))
    (token_grad, prob_grad), gate_grads = lax.scan(one_slot, start_carry, jnp.arange(slot_count, dtype=jnp.int32))
    return (token_grad.astype(jnp.bfloat16), prob_grad.reshape(token_count, top_count), gate_grads.reshape(slot_count * 4, width, quarter))
```

```python
import functools

import jax
import jax.numpy as jnp
from jax import lax
from jax.experimental import pallas as pl
from jax.experimental.pallas import tpu as pltpu
from jax.sharding import PartitionSpec as P

MESH = pl.DeviceIdType.MESH
BF16, F32 = jnp.bfloat16, jnp.float32
NZ, LOCAL, CAP, GROUPS, TOP = 16, 32, 6, 8, 8
CHUNKS, PER = 4, 4
BLOCK = CAP * GROUPS
ROWS = 2 * NZ * CAP
LANES, TOK, FEAT = 128, 96, 64
WIDTH, QUARTER = LOCAL * FEAT, 192
EXTRA = 16
NT = (((1,), (1,)), ((), ()))
TN = (((0,), (0,)), ((), ()))


def along(k):
    odd = lax.rem(k, 2)
    half = lax.div(k + 1, 2)
    return (2 * odd - 1) * half


def dot(a, b, dims=(((1,), (0,)), ((), ()))):
    return lax.dot_general(a, b, dims, preferred_element_type=F32)


def relabel(slots, z, c):
    node = slots >> 3
    o = (z - (node >> 1)) & (NZ - 1)
    o = jnp.where(o > NZ // 2, o - NZ, o)
    k = jnp.where(o > 0, 2 * o - 1, -2 * o)
    return k, (node + c) & 1, slots & 7


def masks(rel, count):
    ids = lax.broadcasted_iota(jnp.int32, (count, LANES), 0)
    named = jnp.zeros((count, LANES), F32)
    for kk in range(TOP):
        named = named + jnp.where(rel[kk : kk + 1, :] == ids, 1.0, 0.0)
    row = lax.broadcasted_iota(jnp.int32, (LANES, LANES), 0)
    col = lax.broadcasted_iota(jnp.int32, (LANES, LANES), 1)
    earlier = jnp.where(row < col, 1.0, 0.0).astype(BF16)
    before = dot(named.astype(BF16), earlier)
    return [jnp.where(before == float(r), named, 0.0) for r in range(CAP)]


def stacked(parts, count):
    return jnp.stack([m.reshape(count // 8, 8, LANES) for m in parts], axis=1).reshape(
        count * CAP, LANES
    )


def kernel(
    tok, grd, prb, slt, wg_hbm, wu_hbm, wd_hbm,
    dtok, dprob, gg_hbm,
    wg, wu, wd, ggv, slot_own, slot_sib, tok_pad, grd_pad,
    send1, recv1, relay, send2, recv2, xs, gs, send3, recv3, zs, ptab,
    send4, recv4, sendx, recvx, home_own, home_sib,
    w_sem, gg_sem, sib_sem, s1, r1, s2, r2, s3, r3, s4, r4, x_sem,
):
    node, loc = lax.axis_index("node"), lax.axis_index("local")
    z, c = lax.div(node, 2), lax.rem(node, 2)
    sibling = 2 * z + lax.rem(c + 1, 2)

    def z_at(distance):
        return lax.rem(z + distance + NZ, NZ)

    weight_copies = [
        pltpu.make_async_copy(src.at[0], dst, w_sem.at[i])
        for i, (src, dst) in enumerate(((wg_hbm, wg), (wu_hbm, wu), (wd_hbm, wd)))
    ]
    for copy in weight_copies:
        copy.start()

    barrier = pltpu.get_barrier_semaphore()

    @pl.loop(1, 2 * NZ)
    def _(p):
        pl.semaphore_signal(
            barrier, inc=1, device_id=(lax.rem(node + p, 2 * NZ), loc), device_id_type=MESH
        )

    @pl.loop(1, LOCAL)
    def _(p):
        pl.semaphore_signal(
            barrier, inc=1, device_id=(node, lax.rem(loc + p, LOCAL)), device_id_type=MESH
        )

    slot_own[...] = jnp.full((TOP, LANES), -1, jnp.int32)
    slot_own[:, :TOK] = slt[...]
    own_slots = slot_own[...]
    k, j, g = relabel(own_slots, z, c)
    rel = jnp.where(own_slots < 0, -1, (k >> 2) * 64 + j * 32 + (k & 3) * 8 + g)
    rel0 = jnp.where((own_slots < 0) | (j > 0), -1, k * 8 + g)
    weights = jnp.concatenate(
        [prb[...].astype(F32), jnp.zeros((TOP, LANES - TOK), F32)], axis=1
    )
    count = 2 * NZ * GROUPS
    parts = masks(rel, count)
    ids = lax.broadcasted_iota(jnp.int32, (count, LANES), 0)
    scale = jnp.zeros((count, LANES), F32)
    for kk in range(TOP):
        scale = scale + jnp.where(rel[kk : kk + 1, :] == ids, weights[kk : kk + 1, :], 0.0)
    pick = stacked(parts, count)
    pick_scaled = stacked([m * scale for m in parts], count)
    tok_pad[...] = jnp.zeros((2 * FEAT, LANES), BF16)
    grd_pad[...] = jnp.zeros((2 * FEAT, LANES), BF16)
    tok_pad[:FEAT, :TOK] = tok[...]
    grd_pad[FEAT:, :TOK] = grd[...]
    rows = dot(pick.astype(BF16), tok_pad[...], NT) + dot(
        pick_scaled.astype(BF16), grd_pad[...], NT
    )
    send1[...] = rows.astype(BF16).reshape(2 * NZ, BLOCK, LANES)

    pl.semaphore_wait(barrier, 2 * NZ - 1 + LOCAL - 1)

    def block_of(k, j):
        return lax.div(k, PER) * (2 * PER) + j * PER + lax.rem(k, PER)

    sib_copy = pltpu.make_async_remote_copy(
        slot_own, slot_sib, sib_sem.at[0], sib_sem.at[1],
        device_id=(sibling, loc), device_id_type=MESH,
    )
    own1 = pltpu.make_async_copy(send1.at[0], recv1.at[0], r1.at[0])
    own1.start()

    @pl.loop(1, 2 * NZ)
    def _(t):
        k, j = lax.div(t, 2), lax.rem(t, 2)
        b = block_of(k, j)
        to = 2 * z_at(-along(k)) + lax.rem(c + j, 2)
        pltpu.make_async_remote_copy(
            send1.at[b], recv1.at[b], s1, r1.at[lax.div(k, PER)],
            device_id=(to, loc), device_id_type=MESH,
        ).start()

    sib_copy.start()

    for i in range(CHUNKS):
        chunk = recv1.at[pl.ds(8 * i, 8)]
        pltpu.make_async_copy(chunk, chunk, r1.at[i]).wait()
        relay[...] = chunk[...].reshape(8 * BLOCK, LANES).astype(F32)
        for g in range(GROUPS):
            send2[i, g] = relay[pl.ds(g, BLOCK, stride=8), :].astype(BF16)
        pltpu.make_async_copy(
            send2.at[i, lax.div(loc, 4)], recv2.at[i, loc], r2.at[i]
        ).start()

        @pl.loop(1, LOCAL)
        def _(p):
            to = lax.rem(loc + p, LOCAL)
            pltpu.make_async_remote_copy(
                send2.at[i, lax.div(to, 4)], recv2.at[i, loc], s2.at[i], r2.at[i],
                device_id=(node, to), device_id_type=MESH,
            ).start()

    home_own[...] = stacked(masks(rel0, NZ * GROUPS), NZ * GROUPS).astype(BF16)
    sib_copy.wait()
    sib_slots = slot_sib[...]
    k, j, g = relabel(sib_slots, z, c)
    rel1 = jnp.where((sib_slots < 0) | (j > 0), -1, k * 8 + g)
    home_sib[...] = stacked(masks(rel1, NZ * GROUPS), NZ * GROUPS).astype(BF16)
    send3[:, TOK:, :] = jnp.zeros((LOCAL, EXTRA, LANES), BF16)

    for copy in weight_copies:
        copy.wait()
    for i in range(CHUNKS):
        pltpu.make_async_copy(recv2.at[i], recv2.at[i], r2.at[i]).wait()
        here = slice(BLOCK * i, BLOCK * (i + 1))
        for p in range(LOCAL // 2):
            a, b = recv2[i, 2 * p], recv2[i, 2 * p + 1]
            there = slice(LANES * p, LANES * (p + 1))
            xs[here, there] = jnp.concatenate([a[:, :FEAT], b[:, :FEAT]], axis=1)
            gs[here, there] = jnp.concatenate([a[:, FEAT:], b[:, FEAT:]], axis=1)

    gate = dot(xs[...], wg[...], NT)
    up = dot(xs[...], wu[...], NT)
    d_hidden = dot(gs[...], wd[...], NT)
    sig = jax.nn.sigmoid(gate)
    silu = gate * sig
    hidden = (silu * up).astype(BF16).astype(F32)
    d_gate = (d_hidden * up * (sig * (1.0 + gate * (1.0 - sig)))).astype(BF16)
    d_up = (d_hidden * silu).astype(BF16)

    def halves(v):
        lower = [v[BLOCK * i : BLOCK * i + BLOCK // 2] for i in range(CHUNKS)]
        upper = [v[BLOCK * i + BLOCK // 2 : BLOCK * (i + 1)] for i in range(CHUNKS)]
        return jnp.concatenate(lower, axis=0), jnp.concatenate(upper, axis=0)

    ones = jnp.ones((8, QUARTER), F32)
    terms = []
    for half in halves(hidden * d_hidden):
        full = jnp.concatenate([half, jnp.zeros((LANES - TOK, QUARTER), F32)], axis=0)
        terms.append(
            lax.dot_general(
                ones, full, NT, precision=lax.Precision.HIGHEST, preferred_element_type=F32
            )[:1]
        )
    high = [t.astype(BF16) for t in terms]
    low = [(t - h.astype(F32)).astype(BF16) for t, h in zip(terms, high)]
    extra = jnp.concatenate(
        [v.astype(F32) for v in high + low] + [jnp.zeros((EXTRA - 4, LANES), F32)], axis=0
    ).astype(BF16)

    @pl.loop(0, LOCAL)
    def _(l):
        send3[l, TOK:, :] = extra

    for p in range(LOCAL // 4):
        there = slice(256 * p, 256 * (p + 1))
        part = dot(d_gate, wg[:, there]) + dot(d_up, wu[:, there])
        lower, upper = halves(part)
        lower, upper = lower.astype(BF16), upper.astype(BF16)
        for q in range(4):
            f = slice(FEAT * q, FEAT * (q + 1))
            send3[4 * p + q, :TOK, :] = jnp.concatenate([lower[:, f], upper[:, f]], axis=1)

    pltpu.make_async_copy(send3.at[loc], recv3.at[loc], r3.at[lax.div(loc, 4)]).start()

    @pl.loop(1, LOCAL)
    def _(p):
        to = lax.rem(loc + p, LOCAL)
        pltpu.make_async_remote_copy(
            send3.at[to], recv3.at[loc], s3, r3.at[lax.div(loc, 4)],
            device_id=(node, to), device_id_type=MESH,
        ).start()

    for p in range(LOCAL // 4):
        there = slice(256 * p, 256 * (p + 1))
        ggv[:, there] = dot(d_gate, xs[:, there], TN).astype(BF16)
    gg_copy = pltpu.make_async_copy(ggv, gg_hbm.at[0], gg_sem)
    gg_copy.start()

    for g in range(GROUPS):
        four = recv3.at[pl.ds(4 * g, 4)]
        pltpu.make_async_copy(four, four, r3.at[g]).wait()
        total = jnp.sum(four[...].astype(F32), axis=0)
        zs[pl.ds(g, TOK, stride=8), :] = total[:TOK]
        prob = total[TOK : TOK + 2] + total[TOK + 2 : TOK + 4]
        ptab[g : g + 1, :] = prob[:1]
        ptab[GROUPS + g : GROUPS + g + 1, :] = prob[1:]
    table = ptab[...].astype(BF16)
    send4[:, :BLOCK, :] = zs[...].reshape(NZ, BLOCK, LANES).astype(BF16)

    @pl.loop(0, NZ)
    def _(k):
        send4[k, BLOCK:, :] = table

    pltpu.make_async_copy(send4.at[0], recv4.at[0], r4).start()

    @pl.loop(1, NZ)
    def _(k):
        pltpu.make_async_remote_copy(
            send4.at[k], recv4.at[k], s4, r4,
            device_id=(2 * z_at(along(k)) + c, loc), device_id_type=MESH,
        ).start()

    pltpu.make_async_copy(recv4, recv4, r4).wait()
    back = recv4[:, :BLOCK, :].reshape(NZ * BLOCK, LANES)

    def prob_rows(home, names, first):
        sums = [jnp.zeros((8, LANES), F32) for _ in range(TOP)]
        groups = lax.broadcasted_iota(jnp.int32, (8, LANES), 0)
        for k in range(NZ):
            values = recv4[k, BLOCK:, :].astype(F32)[first : first + 8]
            hot = home[BLOCK * k : BLOCK * (k + 1), :].astype(F32).reshape(CAP, 8, LANES)
            found = jnp.zeros((8, LANES), F32)
            for r in range(CAP):
                found = found + hot[r] * values[:, CAP * k + r : CAP * k + r + 1]
            for kk in range(TOP):
                sums[kk] = sums[kk] + jnp.where(
                    names[kk : kk + 1, :] == groups + 8 * k, found, 0.0
                )
        return jnp.concatenate([jnp.sum(s, axis=0, keepdims=True) for s in sums], axis=0)

    sendx[:FEAT, :] = dot(back, home_sib[...], TN)[FEAT:]
    sendx[FEAT:, :] = prob_rows(home_sib, rel1, 8)
    x_copy = pltpu.make_async_remote_copy(
        sendx, recvx, x_sem.at[0], x_sem.at[1], device_id=(sibling, loc), device_id_type=MESH
    )
    x_copy.start()
    mine = dot(back, home_own[...], TN)[:FEAT]
    probs_mine = prob_rows(home_own, rel0, 0)
    x_copy.wait()
    dtok[...] = (mine + recvx[:FEAT, :])[:, :TOK].astype(BF16)
    dprob[...] = (probs_mine + recvx[FEAT:, :])[:, :TOK] / prb[...].astype(F32)

    sent = recv1.at[pl.ds(0, 2 * NZ - 1)]
    pltpu.make_async_copy(sent, sent, s1).wait()
    for i in range(CHUNKS):
        sent = recv2.at[i, pl.ds(0, LOCAL - 1)]
        pltpu.make_async_copy(sent, sent, s2.at[i]).wait()
    sent = recv3.at[pl.ds(0, LOCAL - 1)]
    pltpu.make_async_copy(sent, sent, s3).wait()
    sent = recv4.at[pl.ds(0, NZ - 1)]
    pltpu.make_async_copy(sent, sent, s4).wait()
    gg_copy.wait()


def body(tokens, grad_out, probs, slot_of, w_gate, w_up, w_down):
    vmem, hbm = pl.BlockSpec(memory_space=pltpu.VMEM), pl.BlockSpec(memory_space=pl.ANY)
    dma = pltpu.SemaphoreType.DMA
    d_tokens, d_probs, gate_grad = pl.pallas_call(
        kernel,
        out_shape=(
            jax.ShapeDtypeStruct((FEAT, TOK), BF16),
            jax.ShapeDtypeStruct((TOP, TOK), F32),
            jax.ShapeDtypeStruct((1, QUARTER, WIDTH), BF16),
        ),
        in_specs=[vmem] * 4 + [hbm] * 3,
        out_specs=(vmem, vmem, hbm),
        scratch_shapes=[
            pltpu.VMEM((QUARTER, WIDTH), BF16),
            pltpu.VMEM((QUARTER, WIDTH), BF16),
            pltpu.VMEM((QUARTER, WIDTH), BF16),
            pltpu.VMEM((QUARTER, WIDTH), BF16),
            pltpu.VMEM((TOP, LANES), jnp.int32),
            pltpu.VMEM((TOP, LANES), jnp.int32),
            pltpu.VMEM((2 * FEAT, LANES), BF16),
            pltpu.VMEM((2 * FEAT, LANES), BF16),
            pltpu.VMEM((2 * NZ, BLOCK, LANES), BF16),
            pltpu.VMEM((2 * NZ, BLOCK, LANES), BF16),
            pltpu.VMEM((8 * BLOCK, LANES), F32),
            pltpu.VMEM((CHUNKS, GROUPS, BLOCK, LANES), BF16),
            pltpu.VMEM((CHUNKS, LOCAL, BLOCK, LANES), BF16),
            pltpu.VMEM((ROWS, WIDTH), BF16),
            pltpu.VMEM((ROWS, WIDTH), BF16),
            pltpu.VMEM((LOCAL, TOK + EXTRA, LANES), BF16),
            pltpu.VMEM((LOCAL, TOK + EXTRA, LANES), BF16),
            pltpu.VMEM((NZ * BLOCK, LANES), F32),
            pltpu.VMEM((2 * GROUPS, LANES), F32),
            pltpu.VMEM((NZ, BLOCK + EXTRA, LANES), BF16),
            pltpu.VMEM((NZ, BLOCK + EXTRA, LANES), BF16),
            pltpu.VMEM((FEAT + TOP, LANES), F32),
            pltpu.VMEM((FEAT + TOP, LANES), F32),
            pltpu.VMEM((NZ * BLOCK, LANES), BF16),
            pltpu.VMEM((NZ * BLOCK, LANES), BF16),
            dma((3,)),
            dma,
            dma((2,)),
            dma,
            dma((CHUNKS,)),
            dma((CHUNKS,)),
            dma((CHUNKS,)),
            dma,
            dma((GROUPS,)),
            dma,
            dma,
            dma((2,)),
        ],
        compiler_params=pltpu.CompilerParams(
            collective_id=0, has_side_effects=True, vmem_limit_bytes=60 * 1024 * 1024
        ),
    )(
        tokens.T, grad_out.T, probs.T, slot_of.T,
        jnp.swapaxes(w_gate, 1, 2), jnp.swapaxes(w_up, 1, 2), w_down,
    )
    return d_tokens.T, d_probs.T, jnp.swapaxes(gate_grad, 1, 2)


def solution(mesh):
    in_specs = (
        P("node", "local"),
        P("node", "local"),
        P("node", None),
        P("node", None),
        P(("node", "local"), None, None),
        P(("node", "local"), None, None),
        P(("node", "local"), None, None),
    )
    out_specs = (P("node", "local"), P("node", None), P(("node", "local"), None, None))
    return jax.shard_map(body, mesh=mesh, in_specs=in_specs, out_specs=out_specs, check_vma=False)
```

```python
import functools

import jax
import jax.numpy as jnp
from jax import lax
from jax.experimental import pallas as pl
from jax.experimental.pallas import tpu as pltpu
from jax.sharding import PartitionSpec as P

MESH = pl.DeviceIdType.MESH
BF16, F32 = jnp.bfloat16, jnp.float32
NZ, LOCAL, CAP, GROUPS, TOP = 16, 32, 6, 8, 8
CHUNKS, PER = 4, 4
BLOCK = CAP * GROUPS
ROWS = 2 * NZ * CAP
NX, NY = 4, 8
LANES, TOK, FEAT = 128, 96, 64
WIDTH, QUARTER = LOCAL * FEAT, 192
NT = (((1,), (1,)), ((), ()))
TN = (((0,), (0,)), ((), ()))


def along(k):
    odd = lax.rem(k, 2)
    half = lax.div(k + 1, 2)
    return (2 * odd - 1) * half


def dot(a, b, dims=(((1,), (0,)), ((), ()))):
    return lax.dot_general(a, b, dims, preferred_element_type=F32)


def relabel(slots, z, c):
    node = slots >> 3
    o = (z - (node >> 1)) & (NZ - 1)
    o = jnp.where(o > NZ // 2, o - NZ, o)
    k = jnp.where(o > 0, 2 * o - 1, -2 * o)
    return k, (node + c) & 1, slots & 7


def masks(rel, count):
    ids = lax.broadcasted_iota(jnp.int32, (count, LANES), 0)
    named = jnp.zeros((count, LANES), F32)
    for kk in range(TOP):
        named = named + jnp.where(rel[kk : kk + 1, :] == ids, 1.0, 0.0)
    row = lax.broadcasted_iota(jnp.int32, (LANES, LANES), 0)
    col = lax.broadcasted_iota(jnp.int32, (LANES, LANES), 1)
    earlier = jnp.where(row < col, 1.0, 0.0).astype(BF16)
    before = dot(named.astype(BF16), earlier)
    return [jnp.where(before == float(r), named, 0.0) for r in range(CAP)]


def stacked(parts, count):
    return jnp.stack([m.reshape(count // 8, 8, LANES) for m in parts], axis=1).reshape(
        count * CAP, LANES
    )


def kernel(
    tok, grd, prb, slt, wg_hbm, wu_hbm, wd_hbm,
    dtok, dprob, gg_hbm,
    wg, wu, wd, ggv, slot_own, slot_sib, tok_pad, grd_pad,
    send1, recv1, relay, send2, recv2, xs, gs, send3, recvw, sendf, recv3, zs,
    send4, recv4, sendx, recvx, home_own, home_sib, pown, pz, psum, pall, ptab,
    w_sem, gg_sem, sib_sem, s1, r1, s2f, s2d, s2w, r2f, r2d, r2w,
    s3d, s3w, s3f, r3w, r3, s4, r4, x_sem, spz, rpz, spa, rpa,
):
    node, loc = lax.axis_index("node"), lax.axis_index("local")
    z, c = lax.div(node, 2), lax.rem(node, 2)
    sibling = 2 * z + lax.rem(c + 1, 2)
    x, y = lax.div(loc, NY), lax.rem(loc, NY)
    h, m = lax.div(y, 4), lax.rem(y, 4)
    m_low, m_high = lax.rem(m, 2), lax.div(m, 2)
    partner = loc + 1 - 2 * m_low
    pos_f = 3 * (1 - m_low) + 2 * m_high
    pos_w = 3 * m_low + 2 * m_high
    pos_d = 6 * (1 - m_high)

    def place(y_at):
        return lax.rem(y_at + 14 - 4 * h, NY)

    def x_at(distance):
        return lax.rem(x + distance, NX)

    def z_at(distance):
        return lax.rem(z + distance + NZ, NZ)

    weight_copies = [
        pltpu.make_async_copy(src.at[0], dst, w_sem.at[i])
        for i, (src, dst) in enumerate(((wg_hbm, wg), (wu_hbm, wu), (wd_hbm, wd)))
    ]
    for copy in weight_copies:
        copy.start()

    barrier = pltpu.get_barrier_semaphore()

    @pl.loop(1, 2 * NZ)
    def _(p):
        pl.semaphore_signal(
            barrier, inc=1, device_id=(lax.rem(node + p, 2 * NZ), loc), device_id_type=MESH
        )

    @pl.loop(1, LOCAL)
    def _(p):
        pl.semaphore_signal(
            barrier, inc=1, device_id=(node, lax.rem(loc + p, LOCAL)), device_id_type=MESH
        )

    def seen(g):
        return (((g & 1) + h) & 1) * 4 + (g >> 1)

    slot_own[...] = jnp.full((TOP, LANES), -1, jnp.int32)
    slot_own[:, :TOK] = slt[...]
    own_slots = slot_own[...]
    k, j, g = relabel(own_slots, z, c)
    rel = jnp.where(own_slots < 0, -1, (k >> 2) * 64 + j * 32 + (k & 3) * 8 + g)
    rel0 = jnp.where((own_slots < 0) | (j > 0), -1, k * 8 + seen(g))
    weights = jnp.concatenate(
        [prb[...].astype(F32), jnp.zeros((TOP, LANES - TOK), F32)], axis=1
    )
    count = 2 * NZ * GROUPS
    parts = masks(rel, count)
    ids = lax.broadcasted_iota(jnp.int32, (count, LANES), 0)
    scale = jnp.zeros((count, LANES), F32)
    for kk in range(TOP):
        scale = scale + jnp.where(rel[kk : kk + 1, :] == ids, weights[kk : kk + 1, :], 0.0)
    pick = stacked(parts, count)
    pick_scaled = stacked([m * scale for m in parts], count)
    tok_pad[...] = jnp.zeros((2 * FEAT, LANES), BF16)
    grd_pad[...] = jnp.zeros((2 * FEAT, LANES), BF16)
    tok_pad[:FEAT, :TOK] = tok[...]
    grd_pad[FEAT:, :TOK] = grd[...]
    rows = dot(pick.astype(BF16), tok_pad[...], NT) + dot(
        pick_scaled.astype(BF16), grd_pad[...], NT
    )
    send1[...] = rows.astype(BF16).reshape(2 * NZ, BLOCK, LANES)

    pl.semaphore_wait(barrier, 2 * NZ - 1 + LOCAL - 1)

    def block_of(k, j):
        return lax.div(k, PER) * (2 * PER) + j * PER + lax.rem(k, PER)

    sib_copy = pltpu.make_async_remote_copy(
        slot_own, slot_sib, sib_sem.at[0], sib_sem.at[1],
        device_id=(sibling, loc), device_id_type=MESH,
    )
    own1 = pltpu.make_async_copy(send1.at[0], recv1.at[0], r1.at[0])
    own1.start()

    @pl.loop(1, 2 * NZ)
    def _(t):
        k, j = lax.div(t, 2), lax.rem(t, 2)
        b = block_of(k, j)
        to = 2 * z_at(-along(k)) + lax.rem(c + j, 2)
        pltpu.make_async_remote_copy(
            send1.at[b], recv1.at[b], s1, r1.at[lax.div(k, PER)],
            device_id=(to, loc), device_id_type=MESH,
        ).start()

    sib_copy.start()

    def pass_on(i):
        @pl.loop(0, NX)
        def _(d):
            source = x_at(NX - d)
            part = recv2.at[i, source, pl.ds(pos_f, 3)]
            pltpu.make_async_copy(part, part, r2f.at[i, source]).wait()
            pltpu.make_async_remote_copy(
                part, part, s2w.at[i], r2w.at[i],
                device_id=(node, partner), device_id_type=MESH,
            ).start()

    for i in range(CHUNKS):
        chunk = recv1.at[pl.ds(8 * i, 8)]
        pltpu.make_async_copy(chunk, chunk, r1.at[i]).wait()
        relay[...] = chunk[...].reshape(8 * BLOCK, LANES).astype(F32)
        for g in range(GROUPS):
            send2[i, g] = relay[pl.ds(g, BLOCK, stride=8), :].astype(BF16)

        def give(x_to, h_to, member, pos, send_sem, recv_sem):
            pltpu.make_async_remote_copy(
                send2.at[i, 2 * x_to + h_to], recv2.at[i, x, pos], send_sem, recv_sem,
                device_id=(node, NY * x_to + 4 * h_to + member), device_id_type=MESH,
            ).start()

        pos_same, pos_other = lax.rem(m + 6, NY), lax.rem(m + 2, NY)

        @pl.loop(0, NX)
        def _(d):
            to = x_at(d)
            give(to, 1 - h, 3 * (1 - m_high), pos_other, s2f.at[i], r2f.at[i, x])
            give(to, 1 - h, lax.rem(5 - m, 4), pos_other, s2f.at[i], r2f.at[i, x])
            give(to, h, 2 - m_high, pos_same, s2f.at[i], r2f.at[i, x])

        pltpu.make_async_copy(
            send2.at[i, 2 * x + h], recv2.at[i, x, pos_same], r2d.at[i]
        ).start()

        @pl.loop(0, NX)
        def _(d):
            give(x_at(d), h, 2 * m_high + 1 - m_low, pos_same, s2d.at[i], r2d.at[i])

        @pl.loop(1, NX)
        def _(d):
            give(x_at(d), h, m, pos_same, s2d.at[i], r2d.at[i])

        if i > 0:
            pass_on(i - 1)
    pass_on(CHUNKS - 1)

    home_own[...] = stacked(masks(rel0, NZ * GROUPS), NZ * GROUPS).astype(BF16)
    sib_copy.wait()
    sib_slots = slot_sib[...]
    k, j, g = relabel(sib_slots, z, c)
    rel1 = jnp.where((sib_slots < 0) | (j > 0), -1, k * 8 + seen(g))
    home_sib[...] = stacked(masks(rel1, NZ * GROUPS), NZ * GROUPS).astype(BF16)

    for copy in weight_copies:
        copy.wait()
    for i in range(CHUNKS):
        part = recv2.at[i, :, pl.ds(pos_d, 2)]
        pltpu.make_async_copy(part, part, r2d.at[i]).wait()
        part = recv2.at[i, :, pl.ds(pos_w, 3)]
        pltpu.make_async_copy(part, part, r2w.at[i]).wait()
        here = slice(BLOCK * i, BLOCK * (i + 1))
        for p in range(LOCAL // 2):
            first = 2 * p % NY
            a = recv2[i, 2 * p // NY, place(first)]
            b = recv2[i, 2 * p // NY, place(first + 1)]
            there = slice(LANES * p, LANES * (p + 1))
            xs[here, there] = jnp.concatenate([a[:, :FEAT], b[:, :FEAT]], axis=1)
            gs[here, there] = jnp.concatenate([a[:, FEAT:], b[:, FEAT:]], axis=1)

    gate = dot(xs[...], wg[...], NT)
    up = dot(xs[...], wu[...], NT)
    d_hidden = dot(gs[...], wd[...], NT)
    sig = jax.nn.sigmoid(gate)
    silu = gate * sig
    hidden = (silu * up).astype(BF16).astype(F32)
    d_gate = (d_hidden * up * (sig * (1.0 + gate * (1.0 - sig)))).astype(BF16)
    d_up = (d_hidden * silu).astype(BF16)

    def halves(v):
        lower = [v[BLOCK * i : BLOCK * i + BLOCK // 2] for i in range(CHUNKS)]
        upper = [v[BLOCK * i + BLOCK // 2 : BLOCK * (i + 1)] for i in range(CHUNKS)]
        return jnp.concatenate(lower, axis=0), jnp.concatenate(upper, axis=0)

    ones = jnp.ones((8, QUARTER), F32)
    terms = []
    for half in halves(hidden * d_hidden):
        full = jnp.concatenate([half, jnp.zeros((LANES - TOK, QUARTER), F32)], axis=0)
        terms.append(
            lax.dot_general(
                ones, full, NT, precision=lax.Precision.HIGHEST, preferred_element_type=F32
            )[:1]
        )
    pown[0:1, :] = terms[0]
    pown[1:2, :] = terms[1]
    pltpu.make_async_copy(pown, pz.at[0], rpz).start()

    @pl.loop(1, NZ)
    def _(k):
        pltpu.make_async_remote_copy(
            pown, pz.at[k], spz, rpz,
            device_id=(2 * z_at(along(k)) + c, loc), device_id_type=MESH,
        ).start()

    for p in range(LOCAL // 4):
        there = slice(256 * p, 256 * (p + 1))
        part = dot(d_gate, wg[:, there]) + dot(d_up, wu[:, there])
        lower, upper = halves(part)
        lower, upper = lower.astype(BF16), upper.astype(BF16)
        for q in range(4):
            f = slice(FEAT * q, FEAT * (q + 1))
            send3[p // 2, place(4 * (p % 2) + q)] = jnp.concatenate(
                [lower[:, f], upper[:, f]], axis=1
            )

    @pl.loop(0, NX)
    def _(d):
        to = x_at(d)
        pltpu.make_async_remote_copy(
            send3.at[to, pl.ds(pos_w, 3)], recvw.at[to], s3w, r3w.at[to],
            device_id=(node, partner), device_id_type=MESH,
        ).start()

    def give_back(src, x_to, y_to, slot, sem, send_sem):
        pltpu.make_async_remote_copy(
            src, recv3.at[slot], send_sem, r3.at[sem],
            device_id=(node, NY * x_to + y_to), device_id_type=MESH,
        ).start()

    pltpu.make_async_copy(
        send3.at[x, pos_d + m_low], recv3.at[3 * x + m_low], r3.at[x]
    ).start()

    @pl.loop(0, NX)
    def _(d):
        to = x_at(d)
        give_back(
            send3.at[to, pos_d + 1 - m_low], to, 4 * h + 2 * m_high + 1 - m_low,
            3 * x + m_low, x, s3d,
        )

    @pl.loop(1, NX)
    def _(d):
        to = x_at(d)
        give_back(send3.at[to, pos_d + m_low], to, y, 3 * x + m_low, x, s3d)

    @pl.loop(0, NX)
    def _(d):
        to = x_at(d)
        pltpu.make_async_copy(recvw.at[to], recvw.at[to], r3w.at[to]).wait()
        for f in range(3):
            own = send3[to, pos_f + f].astype(F32)
            sendf[to, f] = (own + recvw[to, f].astype(F32)).astype(BF16)
        for f in range(3):
            s_to = lax.rem(pos_f + f + 2, NY)
            other = lax.div(s_to, 4)
            slot = (1 - other) * (3 * x + 2) + other * (3 * NX + 2 * x + m_high)
            give_back(
                sendf.at[to, f], to, lax.rem(s_to + 4 * h, NY), slot, NX * other + x, s3f
            )

    for p in range(LOCAL // 4):
        there = slice(256 * p, 256 * (p + 1))
        ggv[:, there] = dot(d_gate, xs[:, there], TN).astype(BF16)
    gg_copy = pltpu.make_async_copy(ggv, gg_hbm.at[0], gg_sem)
    gg_copy.start()

    pltpu.make_async_copy(pz, pz, rpz).wait()
    lane = lax.broadcasted_iota(jnp.int32, (2, LANES), 1)
    found = jnp.zeros((2, LANES), F32)
    for k in range(NZ):
        found = jnp.where((lane >= CAP * k) & (lane < CAP * (k + 1)), pz[k], found)
    psum[...] = found
    pltpu.make_async_copy(psum, pall.at[loc], rpa).start()

    @pl.loop(1, LOCAL)
    def _(p):
        pltpu.make_async_remote_copy(
            psum, pall.at[loc], spa, rpa,
            device_id=(node, lax.rem(loc + p, LOCAL)), device_id_type=MESH,
        ).start()

    for g in range(GROUPS):
        size = 3 if g < NX else 2
        first = 3 * g if g < NX else 3 * NX + 2 * (g - NX)
        part = recv3.at[pl.ds(first, size)]
        pltpu.make_async_copy(part, part, r3.at[g]).wait()
        zs[pl.ds(g, TOK, stride=8), :] = jnp.sum(part[...].astype(F32), axis=0)
    send4[...] = zs[...].reshape(NZ, BLOCK, LANES).astype(BF16)

    pltpu.make_async_copy(send4.at[0], recv4.at[0], r4).start()

    @pl.loop(1, NZ)
    def _(k):
        pltpu.make_async_remote_copy(
            send4.at[k], recv4.at[k], s4, r4,
            device_id=(2 * z_at(along(k)) + c, loc), device_id_type=MESH,
        ).start()

    pltpu.make_async_copy(pall, pall, rpa).wait()
    for g in range(GROUPS):
        at = 4 * (2 * (g % NX) + lax.rem(h + g // NX, 2))
        four = pall[at] + pall[at + 1] + pall[at + 2] + pall[at + 3]
        ptab[g : g + 1, :] = four[:1]
        ptab[GROUPS + g : GROUPS + g + 1, :] = four[1:]


    def prob_rows(home, names, first):
        sums = [jnp.zeros((8, LANES), F32) for _ in range(TOP)]
        groups = lax.broadcasted_iota(jnp.int32, (8, LANES), 0)
        for k in range(NZ):
            values = ptab[first : first + 8, :]
            hot = home[BLOCK * k : BLOCK * (k + 1), :].astype(F32).reshape(CAP, 8, LANES)
            found = jnp.zeros((8, LANES), F32)
            for r in range(CAP):
                found = found + hot[r] * values[:, CAP * k + r : CAP * k + r + 1]
            for kk in range(TOP):
                sums[kk] = sums[kk] + jnp.where(
                    names[kk : kk + 1, :] == groups + 8 * k, found, 0.0
                )
        return jnp.concatenate([jnp.sum(s, axis=0, keepdims=True) for s in sums], axis=0)

    sendx[FEAT:, :] = prob_rows(home_sib, rel1, 8)
    probs_mine = prob_rows(home_own, rel0, 0)

    pltpu.make_async_copy(recv4, recv4, r4).wait()
    back = recv4[...].reshape(NZ * BLOCK, LANES)
    sendx[:FEAT, :] = dot(back, home_sib[...], TN)[FEAT:]
    x_copy = pltpu.make_async_remote_copy(
        sendx, recvx, x_sem.at[0], x_sem.at[1], device_id=(sibling, loc), device_id_type=MESH
    )
    x_copy.start()
    mine = dot(back, home_own[...], TN)[:FEAT]
    x_copy.wait()
    dtok[...] = (mine + recvx[:FEAT, :])[:, :TOK].astype(BF16)
    dprob[...] = (probs_mine + recvx[FEAT:, :])[:, :TOK] / prb[...].astype(F32)

    sent = recv1.at[pl.ds(0, 2 * NZ - 1)]
    pltpu.make_async_copy(sent, sent, s1).wait()
    for i in range(CHUNKS):
        sent = recv2.at[i, :, pl.ds(0, 3)]
        pltpu.make_async_copy(sent, sent, s2f.at[i]).wait()
        pltpu.make_async_copy(sent, sent, s2w.at[i]).wait()
        sent = recv2.at[i, 0, pl.ds(0, 7)]
        pltpu.make_async_copy(sent, sent, s2d.at[i]).wait()
    sent = recv3.at[pl.ds(0, 7)]
    pltpu.make_async_copy(sent, sent, s3d).wait()
    pltpu.make_async_copy(recvw, recvw, s3w).wait()
    pltpu.make_async_copy(sendf, sendf, s3f).wait()
    sent = pz.at[pl.ds(0, NZ - 1)]
    pltpu.make_async_copy(sent, sent, spz).wait()
    sent = pall.at[pl.ds(0, LOCAL - 1)]
    pltpu.make_async_copy(sent, sent, spa).wait()
    sent = recv4.at[pl.ds(0, NZ - 1)]
    pltpu.make_async_copy(sent, sent, s4).wait()
    gg_copy.wait()


def body(tokens, grad_out, probs, slot_of, w_gate, w_up, w_down):
    vmem, hbm = pl.BlockSpec(memory_space=pltpu.VMEM), pl.BlockSpec(memory_space=pl.ANY)
    dma = pltpu.SemaphoreType.DMA
    d_tokens, d_probs, gate_grad = pl.pallas_call(
        kernel,
        out_shape=(
            jax.ShapeDtypeStruct((FEAT, TOK), BF16),
            jax.ShapeDtypeStruct((TOP, TOK), F32),
            jax.ShapeDtypeStruct((1, QUARTER, WIDTH), BF16),
        ),
        in_specs=[vmem] * 4 + [hbm] * 3,
        out_specs=(vmem, vmem, hbm),
        scratch_shapes=[
            pltpu.VMEM((QUARTER, WIDTH), BF16),
            pltpu.VMEM((QUARTER, WIDTH), BF16),
            pltpu.VMEM((QUARTER, WIDTH), BF16),
            pltpu.VMEM((QUARTER, WIDTH), BF16),
            pltpu.VMEM((TOP, LANES), jnp.int32),
            pltpu.VMEM((TOP, LANES), jnp.int32),
            pltpu.VMEM((2 * FEAT, LANES), BF16),
            pltpu.VMEM((2 * FEAT, LANES), BF16),
            pltpu.VMEM((2 * NZ, BLOCK, LANES), BF16),
            pltpu.VMEM((2 * NZ, BLOCK, LANES), BF16),
            pltpu.VMEM((8 * BLOCK, LANES), F32),
            pltpu.VMEM((CHUNKS, GROUPS, BLOCK, LANES), BF16),
            pltpu.VMEM((CHUNKS, NX, NY, BLOCK, LANES), BF16),
            pltpu.VMEM((ROWS, WIDTH), BF16),
            pltpu.VMEM((ROWS, WIDTH), BF16),
            pltpu.VMEM((NX, NY, TOK, LANES), BF16),
            pltpu.VMEM((NX, 3, TOK, LANES), BF16),
            pltpu.VMEM((NX, 3, TOK, LANES), BF16),
            pltpu.VMEM((5 * NX, TOK, LANES), BF16),
            pltpu.VMEM((NZ * BLOCK, LANES), F32),
            pltpu.VMEM((NZ, BLOCK, LANES), BF16),
            pltpu.VMEM((NZ, BLOCK, LANES), BF16),
            pltpu.VMEM((FEAT + TOP, LANES), F32),
            pltpu.VMEM((FEAT + TOP, LANES), F32),
            pltpu.VMEM((NZ * BLOCK, LANES), BF16),
            pltpu.VMEM((NZ * BLOCK, LANES), BF16),
            pltpu.VMEM((2, LANES), F32),
            pltpu.VMEM((NZ, 2, LANES), F32),
            pltpu.VMEM((2, LANES), F32),
            pltpu.VMEM((LOCAL, 2, LANES), F32),
            pltpu.VMEM((2 * GROUPS, LANES), F32),
            dma((3,)),
            dma,
            dma((2,)),
            dma,
            dma((CHUNKS,)),
            dma((CHUNKS,)),
            dma((CHUNKS,)),
            dma((CHUNKS,)),
            dma((CHUNKS, NX)),
            dma((CHUNKS,)),
            dma((CHUNKS,)),
            dma,
            dma,
            dma,
            dma((NX,)),
            dma((GROUPS,)),
            dma,
            dma,
            dma((2,)),
            dma,
            dma,
            dma,
            dma,
        ],
        compiler_params=pltpu.CompilerParams(
            collective_id=0, has_side_effects=True, vmem_limit_bytes=60 * 1024 * 1024
        ),
    )(
        tokens.T, grad_out.T, probs.T, slot_of.T,
        jnp.swapaxes(w_gate, 1, 2), jnp.swapaxes(w_up, 1, 2), w_down,
    )
    return d_tokens.T, d_probs.T, jnp.swapaxes(gate_grad, 1, 2)


def solution(mesh):
    in_specs = (
        P("node", "local"),
        P("node", "local"),
        P("node", None),
        P("node", None),
        P(("node", "local"), None, None),
        P(("node", "local"), None, None),
        P(("node", "local"), None, None),
    )
    out_specs = (P("node", "local"), P("node", None), P(("node", "local"), None, None))
    return jax.shard_map(body, mesh=mesh, in_specs=in_specs, out_specs=out_specs, check_vma=False)
```

```python
import functools

import jax
import jax.numpy as jnp
from jax import lax
from jax.experimental import pallas as pl
from jax.experimental.pallas import tpu as pltpu
from jax.sharding import PartitionSpec as P

MESH = pl.DeviceIdType.MESH
BF16, F32 = jnp.bfloat16, jnp.float32
NZ, LOCAL, CAP, GROUPS, TOP = 16, 32, 6, 8, 8
CHUNKS, PER = 4, 4
BLOCK = CAP * GROUPS
ROWS = 2 * NZ * CAP
NX, NY = 4, 8
META = 16
LANES, TOK, FEAT = 128, 96, 64
WIDTH, QUARTER = LOCAL * FEAT, 192
NT = (((1,), (1,)), ((), ()))
TN = (((0,), (0,)), ((), ()))


def along(k):
    odd = lax.rem(k, 2)
    half = lax.div(k + 1, 2)
    return (2 * odd - 1) * half


def dot(a, b, dims=(((1,), (0,)), ((), ()))):
    return lax.dot_general(a, b, dims, preferred_element_type=F32)


def relabel(slots, z, c):
    node = slots >> 3
    o = (z - (node >> 1)) & (NZ - 1)
    o = jnp.where(o > NZ // 2, o - NZ, o)
    k = jnp.where(o > 0, 2 * o - 1, -2 * o)
    return k, (node + c) & 1, slots & 7


def masks(rel, count):
    ids = lax.broadcasted_iota(jnp.int32, (count, LANES), 0)
    named = jnp.zeros((count, LANES), F32)
    for kk in range(TOP):
        named = named + jnp.where(rel[kk : kk + 1, :] == ids, 1.0, 0.0)
    row = lax.broadcasted_iota(jnp.int32, (LANES, LANES), 0)
    col = lax.broadcasted_iota(jnp.int32, (LANES, LANES), 1)
    earlier = jnp.where(row < col, 1.0, 0.0).astype(BF16)
    before = dot(named.astype(BF16), earlier)
    return [jnp.where(before == float(r), named, 0.0) for r in range(CAP)]


def slot_index(distance):
    return 2 * distance - 1 if distance > 0 else -2 * distance


def stacked(parts, count):
    return jnp.stack([m.reshape(count // 8, 8, LANES) for m in parts], axis=1).reshape(
        count * CAP, LANES
    )


def kernel(
    tok, grd, prb, slt, wg_hbm, wu_hbm, wd_hbm,
    dtok, dprob, gg_hbm,
    wg, wu, wd, ggv, slot_own, prob_own, raw, gath, relay, send2, recv2, xs, gs, send3, recvw, sendf, recv3, zs,
    send4, recv4, sendx, recvx, home_own, home_sib, pown, pz, psum, pall, ptab,
    w_sem, gg_sem, sz, rz, ssib, rsib, s2f, s2d, s2w, r2f, r2d, r2w,
    s3d, s3w, s3f, r3w, r3, s4, r4, x_sem, spz, rpz, spa, rpa,
):
    node, loc = lax.axis_index("node"), lax.axis_index("local")
    z, c = lax.div(node, 2), lax.rem(node, 2)
    sibling = 2 * z + lax.rem(c + 1, 2)
    x, y = lax.div(loc, NY), lax.rem(loc, NY)
    h, m = lax.div(y, 4), lax.rem(y, 4)
    m_low, m_high = lax.rem(m, 2), lax.div(m, 2)
    partner = loc + 1 - 2 * m_low
    pos_f = 3 * (1 - m_low) + 2 * m_high
    pos_w = 3 * m_low + 2 * m_high
    pos_d = 6 * (1 - m_high)

    def place(y_at):
        return lax.rem(y_at + 14 - 4 * h, NY)

    def x_at(distance):
        return lax.rem(x + distance, NX)

    def z_at(distance):
        return lax.rem(z + distance + NZ, NZ)

    weight_copies = [
        pltpu.make_async_copy(src.at[0], dst, w_sem.at[i])
        for i, (src, dst) in enumerate(((wg_hbm, wg), (wu_hbm, wu), (wd_hbm, wd)))
    ]
    for copy in weight_copies:
        copy.start()

    barrier = pltpu.get_barrier_semaphore()

    pl.semaphore_signal(barrier, inc=1, device_id=(sibling, loc), device_id_type=MESH)

    @pl.loop(1, NZ)
    def _(p):
        pl.semaphore_signal(
            barrier, inc=1, device_id=(2 * z_at(p - NZ) + c, loc), device_id_type=MESH
        )

    @pl.loop(1, LOCAL)
    def _(p):
        pl.semaphore_signal(
            barrier, inc=1, device_id=(node, lax.rem(loc + p, LOCAL)), device_id_type=MESH
        )

    def seen(g):
        return (((g & 1) + h) & 1) * 4 + (g >> 1)

    slot_own[...] = jnp.full((TOP, LANES), -1, jnp.int32)
    slot_own[:, :TOK] = slt[...]
    prob_own[...] = jnp.zeros((TOP, LANES), F32)
    prob_own[:, :TOK] = prb[...].astype(F32)
    raw[...] = jnp.zeros((2 * FEAT, LANES), BF16)
    raw[:FEAT, :TOK] = tok[...]
    raw[FEAT:, :TOK] = grd[...]
    row = lax.broadcasted_iota(jnp.int32, (LANES, LANES), 0)
    col = lax.broadcasted_iota(jnp.int32, (LANES, LANES), 1)
    same = jnp.where(row == col, 1.0, 0.0).astype(BF16)
    earlier = jnp.where(row < col, 1.0, 0.0).astype(BF16)
    gath[0, :TOK, :] = dot(same, raw[...], NT)[:TOK].astype(BF16)
    gath[0, TOK:, :] = jnp.concatenate(
        [slot_own[...].astype(F32), prob_own[...]], axis=0
    ).astype(BF16)

    pl.semaphore_wait(barrier, NZ + LOCAL - 1)

    def block_of(k, j):
        return k // PER * (2 * PER) + j * PER + k % PER

    def hand_on(distance, hops):
        src = gath.at[block_of(slot_index(distance), 0)]
        k = slot_index(distance - hops)
        pltpu.make_async_remote_copy(
            src, gath.at[block_of(k, 0)], sz, rz.at[k],
            device_id=(2 * z_at(hops) + c, loc), device_id_type=MESH,
        ).start()

    def hand_over(distance):
        k = slot_index(distance)
        pltpu.make_async_remote_copy(
            gath.at[block_of(k, 0)], gath.at[block_of(k, 1)], ssib, rsib.at[k // PER],
            device_id=(sibling, loc), device_id_type=MESH,
        ).start()

    def arrived(distance):
        k = slot_index(distance)
        block = gath.at[block_of(k, 0)]
        pltpu.make_async_copy(block, block, rz.at[k]).wait()

    hand_over(0)
    for hops in (3, -3, 1, -1, 6, -6):
        hand_on(0, hops)

    steps = (
        ((1, ()), (-1, ()), (3, (1, -1)), (-3, (-1, 1)), (2, ())),
        ((6, (1, -1, -2)), (-6, (-1, 1)), (-2, ()), (4, ())),
        ((-4, ()), (5, ()), (-5, ())),
        ((7, ()), (-7, ()), (8, ())),
    )

    def pick_rows(i):
        want = (lax.broadcasted_iota(jnp.int32, (8, LANES), 0) + 8 * node).astype(F32)
        lane = lax.broadcasted_iota(jnp.int32, (BLOCK, LANES), 1)
        named, scaled = [], []
        for b in range(8):
            meta = gath[8 * i + b, TOK:, :].astype(F32)
            hits, scale = jnp.zeros((8, LANES), F32), jnp.zeros((8, LANES), F32)
            for kk in range(TOP):
                hit = meta[kk : kk + 1, :] == want
                hits = hits + jnp.where(hit, 1.0, 0.0)
                scale = scale + jnp.where(hit, meta[TOP + kk : TOP + kk + 1, :], 0.0)
            named.append(hits)
            scaled.append(scale)
        before = dot(jnp.concatenate(named, axis=0).astype(BF16), earlier)
        for b in range(8):
            rank = before[8 * b : 8 * b + 8]
            plain = [jnp.where(rank == float(r), named[b], 0.0) for r in range(CAP)]
            times = [jnp.where(rank == float(r), scaled[b], 0.0) for r in range(CAP)]
            pick = jnp.concatenate(plain + times, axis=0).astype(BF16)
            both = dot(pick[:, :TOK], gath[8 * i + b, :TOK, :])
            relay[BLOCK * b : BLOCK * (b + 1), :] = jnp.where(
                lane < FEAT, both[:BLOCK], both[BLOCK:]
            )

    def pass_on(i):
        @pl.loop(0, NX)
        def _(d):
            source = x_at(NX - d)
            part = recv2.at[i, source, pl.ds(pos_f, 3)]
            pltpu.make_async_copy(part, part, r2f.at[i, source]).wait()
            pltpu.make_async_remote_copy(
                part, part, s2w.at[i], r2w.at[i],
                device_id=(node, partner), device_id_type=MESH,
            ).start()

    for i in range(CHUNKS):
        for distance, onward in steps[i]:
            arrived(distance)
            for hops in onward:
                hand_on(distance, hops)
            hand_over(distance)
        four = gath.at[pl.ds(8 * i + PER, PER)]
        pltpu.make_async_copy(four, four, rsib.at[i]).wait()
        pick_rows(i)
        for g in range(GROUPS):
            send2[i, g] = relay[pl.ds(g, BLOCK, stride=8), :].astype(BF16)

        def give(x_to, h_to, member, pos, send_sem, recv_sem):
            pltpu.make_async_remote_copy(
                send2.at[i, 2 * x_to + h_to], recv2.at[i, x, pos], send_sem, recv_sem,
                device_id=(node, NY * x_to + 4 * h_to + member), device_id_type=MESH,
            ).start()

        pos_same, pos_other = lax.rem(m + 6, NY), lax.rem(m + 2, NY)

        @pl.loop(0, NX)
        def _(d):
            to = x_at(d)
            give(to, 1 - h, 3 * (1 - m_high), pos_other, s2f.at[i], r2f.at[i, x])
            give(to, 1 - h, lax.rem(5 - m, 4), pos_other, s2f.at[i], r2f.at[i, x])
            give(to, h, 2 - m_high, pos_same, s2f.at[i], r2f.at[i, x])

        pltpu.make_async_copy(
            send2.at[i, 2 * x + h], recv2.at[i, x, pos_same], r2d.at[i]
        ).start()

        @pl.loop(0, NX)
        def _(d):
            give(x_at(d), h, 2 * m_high + 1 - m_low, pos_same, s2d.at[i], r2d.at[i])

        @pl.loop(1, NX)
        def _(d):
            give(x_at(d), h, m, pos_same, s2d.at[i], r2d.at[i])

        if i > 0:
            pass_on(i - 1)
    pass_on(CHUNKS - 1)

    own_slots = slot_own[...]
    k, j, g = relabel(own_slots, z, c)
    rel0 = jnp.where((own_slots < 0) | (j > 0), -1, k * 8 + seen(g))
    home_own[...] = stacked(masks(rel0, NZ * GROUPS), NZ * GROUPS).astype(BF16)
    sib_slots = gath[PER, TOK : TOK + TOP, :].astype(F32).astype(jnp.int32)
    k, j, g = relabel(sib_slots, z, c)
    rel1 = jnp.where((sib_slots < 0) | (j > 0), -1, k * 8 + seen(g))
    home_sib[...] = stacked(masks(rel1, NZ * GROUPS), NZ * GROUPS).astype(BF16)

    for copy in weight_copies:
        copy.wait()
    for i in range(CHUNKS):
        part = recv2.at[i, :, pl.ds(pos_d, 2)]
        pltpu.make_async_copy(part, part, r2d.at[i]).wait()
        part = recv2.at[i, :, pl.ds(pos_w, 3)]
        pltpu.make_async_copy(part, part, r2w.at[i]).wait()
        here = slice(BLOCK * i, BLOCK * (i + 1))
        for p in range(LOCAL // 2):
            first = 2 * p % NY
            a = recv2[i, 2 * p // NY, place(first)]
            b = recv2[i, 2 * p // NY, place(first + 1)]
            there = slice(LANES * p, LANES * (p + 1))
            xs[here, there] = jnp.concatenate([a[:, :FEAT], b[:, :FEAT]], axis=1)
            gs[here, there] = jnp.concatenate([a[:, FEAT:], b[:, FEAT:]], axis=1)

    gate = dot(xs[...], wg[...], NT)
    up = dot(xs[...], wu[...], NT)
    d_hidden = dot(gs[...], wd[...], NT)
    sig = jax.nn.sigmoid(gate)
    silu = gate * sig
    hidden = (silu * up).astype(BF16).astype(F32)
    d_gate = (d_hidden * up * (sig * (1.0 + gate * (1.0 - sig)))).astype(BF16)
    d_up = (d_hidden * silu).astype(BF16)

    def halves(v):
        lower = [v[BLOCK * i : BLOCK * i + BLOCK // 2] for i in range(CHUNKS)]
        upper = [v[BLOCK * i + BLOCK // 2 : BLOCK * (i + 1)] for i in range(CHUNKS)]
        return jnp.concatenate(lower, axis=0), jnp.concatenate(upper, axis=0)

    ones = jnp.ones((8, QUARTER), F32)
    terms = []
    for half in halves(hidden * d_hidden):
        full = jnp.concatenate([half, jnp.zeros((LANES - TOK, QUARTER), F32)], axis=0)
        terms.append(
            lax.dot_general(
                ones, full, NT, precision=lax.Precision.HIGHEST, preferred_element_type=F32
            )[:1]
        )
    pown[0:1, :] = terms[0]
    pown[1:2, :] = terms[1]
    pltpu.make_async_copy(pown, pz.at[0], rpz).start()

    @pl.loop(1, NZ)
    def _(k):
        pltpu.make_async_remote_copy(
            pown, pz.at[k], spz, rpz,
            device_id=(2 * z_at(along(k)) + c, loc), device_id_type=MESH,
        ).start()

    for p in range(LOCAL // 4):
        there = slice(256 * p, 256 * (p + 1))
        part = dot(d_gate, wg[:, there]) + dot(d_up, wu[:, there])
        lower, upper = halves(part)
        lower, upper = lower.astype(BF16), upper.astype(BF16)
        for q in range(4):
            f = slice(FEAT * q, FEAT * (q + 1))
            send3[p // 2, place(4 * (p % 2) + q)] = jnp.concatenate(
                [lower[:, f], upper[:, f]], axis=1
            )

    @pl.loop(0, NX)
    def _(d):
        to = x_at(d)
        pltpu.make_async_remote_copy(
            send3.at[to, pl.ds(pos_w, 3)], recvw.at[to], s3w, r3w.at[to],
            device_id=(node, partner), device_id_type=MESH,
        ).start()

    def give_back(src, x_to, y_to, slot, sem, send_sem):
        pltpu.make_async_remote_copy(
            src, recv3.at[slot], send_sem, r3.at[sem],
            device_id=(node, NY * x_to + y_to), device_id_type=MESH,
        ).start()

    pltpu.make_async_copy(
        send3.at[x, pos_d + m_low], recv3.at[3 * x + m_low], r3.at[x]
    ).start()

    @pl.loop(0, NX)
    def _(d):
        to = x_at(d)
        give_back(
            send3.at[to, pos_d + 1 - m_low], to, 4 * h + 2 * m_high + 1 - m_low,
            3 * x + m_low, x, s3d,
        )

    @pl.loop(1, NX)
    def _(d):
        to = x_at(d)
        give_back(send3.at[to, pos_d + m_low], to, y, 3 * x + m_low, x, s3d)

    @pl.loop(0, NX)
    def _(d):
        to = x_at(d)
        pltpu.make_async_copy(recvw.at[to], recvw.at[to], r3w.at[to]).wait()
        for f in range(3):
            own = send3[to, pos_f + f].astype(F32)
            sendf[to, f] = (own + recvw[to, f].astype(F32)).astype(BF16)
        for f in range(3):
            s_to = lax.rem(pos_f + f + 2, NY)
            other = lax.div(s_to, 4)
            slot = (1 - other) * (3 * x + 2) + other * (3 * NX + 2 * x + m_high)
            give_back(
                sendf.at[to, f], to, lax.rem(s_to + 4 * h, NY), slot, NX * other + x, s3f
            )

    for p in range(LOCAL // 4):
        there = slice(256 * p, 256 * (p + 1))
        ggv[:, there] = dot(d_gate, xs[:, there], TN).astype(BF16)
    gg_copy = pltpu.make_async_copy(ggv, gg_hbm.at[0], gg_sem)
    gg_copy.start()

    pltpu.make_async_copy(pz, pz, rpz).wait()
    lane = lax.broadcasted_iota(jnp.int32, (2, LANES), 1)
    found = jnp.zeros((2, LANES), F32)
    for k in range(NZ):
        found = jnp.where((lane >= CAP * k) & (lane < CAP * (k + 1)), pz[k], found)
    psum[...] = found
    pltpu.make_async_copy(psum, pall.at[loc], rpa).start()

    @pl.loop(1, LOCAL)
    def _(p):
        pltpu.make_async_remote_copy(
            psum, pall.at[loc], spa, rpa,
            device_id=(node, lax.rem(loc + p, LOCAL)), device_id_type=MESH,
        ).start()

    for g in range(GROUPS):
        size = 3 if g < NX else 2
        first = 3 * g if g < NX else 3 * NX + 2 * (g - NX)
        part = recv3.at[pl.ds(first, size)]
        pltpu.make_async_copy(part, part, r3.at[g]).wait()
        zs[pl.ds(g, TOK, stride=8), :] = jnp.sum(part[...].astype(F32), axis=0)
    send4[...] = zs[...].reshape(NZ, BLOCK, LANES).astype(BF16)

    pltpu.make_async_copy(send4.at[0], recv4.at[0], r4).start()

    @pl.loop(1, NZ)
    def _(k):
        pltpu.make_async_remote_copy(
            send4.at[k], recv4.at[k], s4, r4,
            device_id=(2 * z_at(along(k)) + c, loc), device_id_type=MESH,
        ).start()

    pltpu.make_async_copy(pall, pall, rpa).wait()
    for g in range(GROUPS):
        at = 4 * (2 * (g % NX) + lax.rem(h + g // NX, 2))
        four = pall[at] + pall[at + 1] + pall[at + 2] + pall[at + 3]
        ptab[g : g + 1, :] = four[:1]
        ptab[GROUPS + g : GROUPS + g + 1, :] = four[1:]


    def prob_rows(home, names, first):
        sums = [jnp.zeros((8, LANES), F32) for _ in range(TOP)]
        groups = lax.broadcasted_iota(jnp.int32, (8, LANES), 0)
        for k in range(NZ):
            values = ptab[first : first + 8, :]
            hot = home[BLOCK * k : BLOCK * (k + 1), :].astype(F32).reshape(CAP, 8, LANES)
            found = jnp.zeros((8, LANES), F32)
            for r in range(CAP):
                found = found + hot[r] * values[:, CAP * k + r : CAP * k + r + 1]
            for kk in range(TOP):
                sums[kk] = sums[kk] + jnp.where(
                    names[kk : kk + 1, :] == groups + 8 * k, found, 0.0
                )
        return jnp.concatenate([jnp.sum(s, axis=0, keepdims=True) for s in sums], axis=0)

    sendx[FEAT:, :] = prob_rows(home_sib, rel1, 8)
    probs_mine = prob_rows(home_own, rel0, 0)

    pltpu.make_async_copy(recv4, recv4, r4).wait()
    back = recv4[...].reshape(NZ * BLOCK, LANES)
    sendx[:FEAT, :] = dot(back, home_sib[...], TN)[FEAT:]
    x_copy = pltpu.make_async_remote_copy(
        sendx, recvx, x_sem.at[0], x_sem.at[1], device_id=(sibling, loc), device_id_type=MESH
    )
    x_copy.start()
    mine = dot(back, home_own[...], TN)[:FEAT]
    x_copy.wait()
    dtok[...] = (mine + recvx[:FEAT, :])[:, :TOK].astype(BF16)
    dprob[...] = (probs_mine + recvx[FEAT:, :])[:, :TOK] / prb[...].astype(F32)

    sent = gath.at[pl.ds(0, NZ - 1)]
    pltpu.make_async_copy(sent, sent, sz).wait()
    sent = gath.at[pl.ds(0, NZ)]
    pltpu.make_async_copy(sent, sent, ssib).wait()
    for i in range(CHUNKS):
        sent = recv2.at[i, :, pl.ds(0, 3)]
        pltpu.make_async_copy(sent, sent, s2f.at[i]).wait()
        pltpu.make_async_copy(sent, sent, s2w.at[i]).wait()
        sent = recv2.at[i, 0, pl.ds(0, 7)]
        pltpu.make_async_copy(sent, sent, s2d.at[i]).wait()
    sent = recv3.at[pl.ds(0, 7)]
    pltpu.make_async_copy(sent, sent, s3d).wait()
    pltpu.make_async_copy(recvw, recvw, s3w).wait()
    pltpu.make_async_copy(sendf, sendf, s3f).wait()
    sent = pz.at[pl.ds(0, NZ - 1)]
    pltpu.make_async_copy(sent, sent, spz).wait()
    sent = pall.at[pl.ds(0, LOCAL - 1)]
    pltpu.make_async_copy(sent, sent, spa).wait()
    sent = recv4.at[pl.ds(0, NZ - 1)]
    pltpu.make_async_copy(sent, sent, s4).wait()
    gg_copy.wait()


def body(tokens, grad_out, probs, slot_of, w_gate, w_up, w_down):
    vmem, hbm = pl.BlockSpec(memory_space=pltpu.VMEM), pl.BlockSpec(memory_space=pl.ANY)
    dma = pltpu.SemaphoreType.DMA
    d_tokens, d_probs, gate_grad = pl.pallas_call(
        kernel,
        out_shape=(
            jax.ShapeDtypeStruct((FEAT, TOK), BF16),
            jax.ShapeDtypeStruct((TOP, TOK), F32),
            jax.ShapeDtypeStruct((1, QUARTER, WIDTH), BF16),
        ),
        in_specs=[vmem] * 4 + [hbm] * 3,
        out_specs=(vmem, vmem, hbm),
        scratch_shapes=[
            pltpu.VMEM((QUARTER, WIDTH), BF16),
            pltpu.VMEM((QUARTER, WIDTH), BF16),
            pltpu.VMEM((QUARTER, WIDTH), BF16),
            pltpu.VMEM((QUARTER, WIDTH), BF16),
            pltpu.VMEM((TOP, LANES), jnp.int32),
            pltpu.VMEM((TOP, LANES), F32),
            pltpu.VMEM((2 * FEAT, LANES), BF16),
            pltpu.VMEM((2 * NZ, TOK + META, LANES), BF16),
            pltpu.VMEM((8 * BLOCK, LANES), F32),
            pltpu.VMEM((CHUNKS, GROUPS, BLOCK, LANES), BF16),
            pltpu.VMEM((CHUNKS, NX, NY, BLOCK, LANES), BF16),
            pltpu.VMEM((ROWS, WIDTH), BF16),
            pltpu.VMEM((ROWS, WIDTH), BF16),
            pltpu.VMEM((NX, NY, TOK, LANES), BF16),
            pltpu.VMEM((NX, 3, TOK, LANES), BF16),
            pltpu.VMEM((NX, 3, TOK, LANES), BF16),
            pltpu.VMEM((5 * NX, TOK, LANES), BF16),
            pltpu.VMEM((NZ * BLOCK, LANES), F32),
            pltpu.VMEM((NZ, BLOCK, LANES), BF16),
            pltpu.VMEM((NZ, BLOCK, LANES), BF16),
            pltpu.VMEM((FEAT + TOP, LANES), F32),
            pltpu.VMEM((FEAT + TOP, LANES), F32),
            pltpu.VMEM((NZ * BLOCK, LANES), BF16),
            pltpu.VMEM((NZ * BLOCK, LANES), BF16),
            pltpu.VMEM((2, LANES), F32),
            pltpu.VMEM((NZ, 2, LANES), F32),
            pltpu.VMEM((2, LANES), F32),
            pltpu.VMEM((LOCAL, 2, LANES), F32),
            pltpu.VMEM((2 * GROUPS, LANES), F32),
            dma((3,)),
            dma,
            dma,
            dma((NZ,)),
            dma,
            dma((CHUNKS,)),
            dma((CHUNKS,)),
            dma((CHUNKS,)),
            dma((CHUNKS,)),
            dma((CHUNKS, NX)),
            dma((CHUNKS,)),
            dma((CHUNKS,)),
            dma,
            dma,
            dma,
            dma((NX,)),
            dma((GROUPS,)),
            dma,
            dma,
            dma((2,)),
            dma,
            dma,
            dma,
            dma,
        ],
        compiler_params=pltpu.CompilerParams(
            collective_id=0, has_side_effects=True, vmem_limit_bytes=60 * 1024 * 1024
        ),
    )(
        tokens.T, grad_out.T, probs.T, slot_of.T,
        jnp.swapaxes(w_gate, 1, 2), jnp.swapaxes(w_up, 1, 2), w_down,
    )
    return d_tokens.T, d_probs.T, jnp.swapaxes(gate_grad, 1, 2)


def solution(mesh):
    in_specs = (
        P("node", "local"),
        P("node", "local"),
        P("node", None),
        P("node", None),
        P(("node", "local"), None, None),
        P(("node", "local"), None, None),
        P(("node", "local"), None, None),
    )
    out_specs = (P("node", "local"), P("node", None), P(("node", "local"), None, None))
    return jax.shard_map(body, mesh=mesh, in_specs=in_specs, out_specs=out_specs, check_vma=False)
```

```python
import functools

import jax
import jax.numpy as jnp
from jax import lax
from jax.experimental import pallas as pl
from jax.experimental.pallas import tpu as pltpu
from jax.sharding import PartitionSpec as P

MESH = pl.DeviceIdType.MESH
BF16, F32 = jnp.bfloat16, jnp.float32
NZ, LOCAL, CAP, GROUPS, TOP = 16, 32, 6, 8, 8
CHUNKS, PER = 4, 4
BLOCK = CAP * GROUPS
ROWS = 2 * NZ * CAP
NX, NY = 4, 8
LANES, TOK, FEAT = 128, 96, 64
WIDTH, QUARTER = LOCAL * FEAT, 192
NT = (((1,), (1,)), ((), ()))
TN = (((0,), (0,)), ((), ()))


def along(k):
    odd = lax.rem(k, 2)
    half = lax.div(k + 1, 2)
    return (2 * odd - 1) * half


def dot(a, b, dims=(((1,), (0,)), ((), ()))):
    return lax.dot_general(a, b, dims, preferred_element_type=F32)


def relabel(slots, z, c):
    node = slots >> 3
    o = (z - (node >> 1)) & (NZ - 1)
    o = jnp.where(o > NZ // 2, o - NZ, o)
    k = jnp.where(o > 0, 2 * o - 1, -2 * o)
    return k, (node + c) & 1, slots & 7


def masks(rel, count):
    ids = lax.broadcasted_iota(jnp.int32, (count, LANES), 0)
    named = jnp.zeros((count, LANES), F32)
    for kk in range(TOP):
        named = named + jnp.where(rel[kk : kk + 1, :] == ids, 1.0, 0.0)
    row = lax.broadcasted_iota(jnp.int32, (LANES, LANES), 0)
    col = lax.broadcasted_iota(jnp.int32, (LANES, LANES), 1)
    earlier = jnp.where(row < col, 1.0, 0.0).astype(BF16)
    before = dot(named.astype(BF16), earlier)
    return [jnp.where(before == float(r), named, 0.0) for r in range(CAP)]


def stacked(parts, count):
    return jnp.stack([m.reshape(count // 8, 8, LANES) for m in parts], axis=1).reshape(
        count * CAP, LANES
    )


def kernel(
    tok, grd, prb, slt, wg_hbm, wu_hbm, wd_hbm,
    small, gg_hbm,
    wg, wu, wd, ggv, slot_own, slot_sib, tok_pad, grd_pad,
    send1, recv1, relay, send2, recv2, xs, gs, send3, recvw, sendf, recv3, zs,
    send4, recv4, sendx, recvx, home_own, home_sib, pown, pz, psum, pall, ptab,
    w_sem, gg_sem, sib_sem, s1, r1, s2f, s2d, s2w, r2f, r2d, r2w,
    s3d, s3w, s3f, r3w, r3, s4, r4, x_sem, spz, rpz, spa, rpa,
):
    node, loc = lax.axis_index("node"), lax.axis_index("local")
    z, c = lax.div(node, 2), lax.rem(node, 2)
    sibling = 2 * z + lax.rem(c + 1, 2)
    x, y = lax.div(loc, NY), lax.rem(loc, NY)
    h, m = lax.div(y, 4), lax.rem(y, 4)
    m_low, m_high = lax.rem(m, 2), lax.div(m, 2)
    partner = loc + 1 - 2 * m_low
    pos_f = 3 * (1 - m_low) + 2 * m_high
    pos_w = 3 * m_low + 2 * m_high
    pos_d = 6 * (1 - m_high)

    def place(y_at):
        return lax.rem(y_at + 14 - 4 * h, NY)

    def x_at(distance):
        return lax.rem(x + distance, NX)

    def z_at(distance):
        return lax.rem(z + distance + NZ, NZ)

    weight_copies = [
        pltpu.make_async_copy(src.at[0], dst, w_sem.at[i])
        for i, (src, dst) in enumerate(((wg_hbm, wg), (wu_hbm, wu), (wd_hbm, wd)))
    ]
    for copy in weight_copies:
        copy.start()

    barrier = pltpu.get_barrier_semaphore()

    @pl.loop(1, 2 * NZ)
    def _(p):
        pl.semaphore_signal(
            barrier, inc=1, device_id=(lax.rem(node + p, 2 * NZ), loc), device_id_type=MESH
        )

    @pl.loop(1, LOCAL)
    def _(p):
        pl.semaphore_signal(
            barrier, inc=1, device_id=(node, lax.rem(loc + p, LOCAL)), device_id_type=MESH
        )

    def seen(g):
        return (((g & 1) + h) & 1) * 4 + (g >> 1)

    slot_own[...] = jnp.full((TOP, LANES), -1, jnp.int32)
    slot_own[:, :TOK] = slt[...]
    own_slots = slot_own[...]
    k, j, g = relabel(own_slots, z, c)
    rel = jnp.where(own_slots < 0, -1, (k >> 2) * 64 + j * 32 + (k & 3) * 8 + g)
    rel0 = jnp.where((own_slots < 0) | (j > 0), -1, k * 8 + seen(g))
    weights = jnp.concatenate(
        [prb[...].astype(F32), jnp.zeros((TOP, LANES - TOK), F32)], axis=1
    )
    count = 2 * NZ * GROUPS
    parts = masks(rel, count)
    ids = lax.broadcasted_iota(jnp.int32, (count, LANES), 0)
    scale = jnp.zeros((count, LANES), F32)
    for kk in range(TOP):
        scale = scale + jnp.where(rel[kk : kk + 1, :] == ids, weights[kk : kk + 1, :], 0.0)
    pick = stacked(parts, count)
    pick_scaled = stacked([m * scale for m in parts], count)
    tok_pad[...] = jnp.zeros((2 * FEAT, LANES), BF16)
    grd_pad[...] = jnp.zeros((2 * FEAT, LANES), BF16)
    tok_pad[:FEAT, :TOK] = tok[...]
    grd_pad[FEAT:, :TOK] = grd[...]
    rows = dot(pick.astype(BF16), tok_pad[...], NT) + dot(
        pick_scaled.astype(BF16), grd_pad[...], NT
    )
    send1[...] = rows.astype(BF16).reshape(2 * NZ, BLOCK, LANES)

    pl.semaphore_wait(barrier, 2 * NZ - 1 + LOCAL - 1)

    def block_of(k, j):
        return lax.div(k, PER) * (2 * PER) + j * PER + lax.rem(k, PER)

    sib_copy = pltpu.make_async_remote_copy(
        slot_own, slot_sib, sib_sem.at[0], sib_sem.at[1],
        device_id=(sibling, loc), device_id_type=MESH,
    )
    own1 = pltpu.make_async_copy(send1.at[0], recv1.at[0], r1.at[0])
    own1.start()

    @pl.loop(1, 2 * NZ)
    def _(t):
        k, j = lax.div(t, 2), lax.rem(t, 2)
        b = block_of(k, j)
        to = 2 * z_at(-along(k)) + lax.rem(c + j, 2)
        pltpu.make_async_remote_copy(
            send1.at[b], recv1.at[b], s1, r1.at[lax.div(k, PER)],
            device_id=(to, loc), device_id_type=MESH,
        ).start()

    sib_copy.start()

    def pass_on(i):
        @pl.loop(0, NX)
        def _(d):
            source = x_at(NX - d)
            part = recv2.at[i, source, pl.ds(pos_f, 3)]
            pltpu.make_async_copy(part, part, r2f.at[i, source]).wait()
            pltpu.make_async_remote_copy(
                part, part, s2w.at[i], r2w.at[i],
                device_id=(node, partner), device_id_type=MESH,
            ).start()

    for i in range(CHUNKS):
        chunk = recv1.at[pl.ds(8 * i, 8)]
        pltpu.make_async_copy(chunk, chunk, r1.at[i]).wait()
        relay[...] = chunk[...].reshape(8 * BLOCK, LANES).astype(F32)
        for g in range(GROUPS):
            send2[i, g] = relay[pl.ds(g, BLOCK, stride=8), :].astype(BF16)

        def give(x_to, h_to, member, pos, send_sem, recv_sem):
            pltpu.make_async_remote_copy(
                send2.at[i, 2 * x_to + h_to], recv2.at[i, x, pos], send_sem, recv_sem,
                device_id=(node, NY * x_to + 4 * h_to + member), device_id_type=MESH,
            ).start()

        pos_same, pos_other = lax.rem(m + 6, NY), lax.rem(m + 2, NY)

        @pl.loop(0, NX)
        def _(d):
            to = x_at(d)
            give(to, 1 - h, 3 * (1 - m_high), pos_other, s2f.at[i], r2f.at[i, x])
            give(to, 1 - h, lax.rem(5 - m, 4), pos_other, s2f.at[i], r2f.at[i, x])
            give(to, h, 2 - m_high, pos_same, s2f.at[i], r2f.at[i, x])

        pltpu.make_async_copy(
            send2.at[i, 2 * x + h], recv2.at[i, x, pos_same], r2d.at[i]
        ).start()

        @pl.loop(0, NX)
        def _(d):
            give(x_at(d), h, 2 * m_high + 1 - m_low, pos_same, s2d.at[i], r2d.at[i])

        @pl.loop(1, NX)
        def _(d):
            give(x_at(d), h, m, pos_same, s2d.at[i], r2d.at[i])

        if i > 0:
            pass_on(i - 1)
    pass_on(CHUNKS - 1)

    home_own[...] = stacked(masks(rel0, NZ * GROUPS), NZ * GROUPS).astype(BF16)
    sib_copy.wait()
    sib_slots = slot_sib[...]
    k, j, g = relabel(sib_slots, z, c)
    rel1 = jnp.where((sib_slots < 0) | (j > 0), -1, k * 8 + seen(g))
    home_sib[...] = stacked(masks(rel1, NZ * GROUPS), NZ * GROUPS).astype(BF16)

    for copy in weight_copies:
        copy.wait()
    for i in range(CHUNKS):
        part = recv2.at[i, :, pl.ds(pos_d, 2)]
        pltpu.make_async_copy(part, part, r2d.at[i]).wait()
        part = recv2.at[i, :, pl.ds(pos_w, 3)]
        pltpu.make_async_copy(part, part, r2w.at[i]).wait()
        here = slice(BLOCK * i, BLOCK * (i + 1))
        for p in range(LOCAL // 2):
            first = 2 * p % NY
            a = recv2[i, 2 * p // NY, place(first)]
            b = recv2[i, 2 * p // NY, place(first + 1)]
            there = slice(LANES * p, LANES * (p + 1))
            xs[here, there] = jnp.concatenate([a[:, :FEAT], b[:, :FEAT]], axis=1)
            gs[here, there] = jnp.concatenate([a[:, FEAT:], b[:, FEAT:]], axis=1)

    gate = dot(xs[...], wg[...], NT)
    up = dot(xs[...], wu[...], NT)
    d_hidden = dot(gs[...], wd[...], NT)
    sig = jax.nn.sigmoid(gate)
    silu = gate * sig
    hidden = (silu * up).astype(BF16).astype(F32)
    d_gate = (d_hidden * up * (sig * (1.0 + gate * (1.0 - sig)))).astype(BF16)
    d_up = (d_hidden * silu).astype(BF16)

    def halves(v):
        lower = [v[BLOCK * i : BLOCK * i + BLOCK // 2] for i in range(CHUNKS)]
        upper = [v[BLOCK * i + BLOCK // 2 : BLOCK * (i + 1)] for i in range(CHUNKS)]
        return jnp.concatenate(lower, axis=0), jnp.concatenate(upper, axis=0)

    ones = jnp.ones((8, QUARTER), F32)
    terms = []
    for half in halves(hidden * d_hidden):
        full = jnp.concatenate([half, jnp.zeros((LANES - TOK, QUARTER), F32)], axis=0)
        terms.append(
            lax.dot_general(
                ones, full, NT, precision=lax.Precision.HIGHEST, preferred_element_type=F32
            )[:1]
        )
    pown[0:1, :] = terms[0]
    pown[1:2, :] = terms[1]
    pltpu.make_async_copy(pown, pz.at[0], rpz).start()

    @pl.loop(1, NZ)
    def _(k):
        pltpu.make_async_remote_copy(
            pown, pz.at[k], spz, rpz,
            device_id=(2 * z_at(along(k)) + c, loc), device_id_type=MESH,
        ).start()

    for p in range(LOCAL // 4):
        there = slice(256 * p, 256 * (p + 1))
        part = dot(d_gate, wg[:, there]) + dot(d_up, wu[:, there])
        lower, upper = halves(part)
        lower, upper = lower.astype(BF16), upper.astype(BF16)
        for q in range(4):
            f = slice(FEAT * q, FEAT * (q + 1))
            send3[p // 2, place(4 * (p % 2) + q)] = jnp.concatenate(
                [lower[:, f], upper[:, f]], axis=1
            )

    @pl.loop(0, NX)
    def _(d):
        to = x_at(d)
        pltpu.make_async_remote_copy(
            send3.at[to, pl.ds(pos_w, 3)], recvw.at[to], s3w, r3w.at[to],
            device_id=(node, partner), device_id_type=MESH,
        ).start()

    def give_back(src, x_to, y_to, slot, sem, send_sem):
        pltpu.make_async_remote_copy(
            src, recv3.at[slot], send_sem, r3.at[sem],
            device_id=(node, NY * x_to + y_to), device_id_type=MESH,
        ).start()

    pltpu.make_async_copy(
        send3.at[x, pos_d + m_low], recv3.at[3 * x + m_low], r3.at[x]
    ).start()

    @pl.loop(0, NX)
    def _(d):
        to = x_at(d)
        give_back(
            send3.at[to, pos_d + 1 - m_low], to, 4 * h + 2 * m_high + 1 - m_low,
            3 * x + m_low, x, s3d,
        )

    @pl.loop(1, NX)
    def _(d):
        to = x_at(d)
        give_back(send3.at[to, pos_d + m_low], to, y, 3 * x + m_low, x, s3d)

    @pl.loop(0, NX)
    def _(d):
        to = x_at(d)
        pltpu.make_async_copy(recvw.at[to], recvw.at[to], r3w.at[to]).wait()
        for f in range(3):
            own = send3[to, pos_f + f].astype(F32)
            sendf[to, f] = (own + recvw[to, f].astype(F32)).astype(BF16)
        for f in range(3):
            s_to = lax.rem(pos_f + f + 2, NY)
            other = lax.div(s_to, 4)
            slot = (1 - other) * (3 * x + 2) + other * (3 * NX + 2 * x + m_high)
            give_back(
                sendf.at[to, f], to, lax.rem(s_to + 4 * h, NY), slot, NX * other + x, s3f
            )

    for p in range(LOCAL // 4):
        there = slice(256 * p, 256 * (p + 1))
        ggv[:, there] = dot(d_gate, xs[:, there], TN).astype(BF16)
    gg_copy = pltpu.make_async_copy(ggv, gg_hbm.at[0], gg_sem)
    gg_copy.start()

    pltpu.make_async_copy(pz, pz, rpz).wait()
    lane = lax.broadcasted_iota(jnp.int32, (2, LANES), 1)
    found = jnp.zeros((2, LANES), F32)
    for k in range(NZ):
        found = jnp.where((lane >= CAP * k) & (lane < CAP * (k + 1)), pz[k], found)
    psum[...] = found
    pltpu.make_async_copy(psum, pall.at[loc], rpa).start()

    @pl.loop(1, LOCAL)
    def _(p):
        pltpu.make_async_remote_copy(
            psum, pall.at[loc], spa, rpa,
            device_id=(node, lax.rem(loc + p, LOCAL)), device_id_type=MESH,
        ).start()

    for g in range(GROUPS):
        size = 3 if g < NX else 2
        first = 3 * g if g < NX else 3 * NX + 2 * (g - NX)
        part = recv3.at[pl.ds(first, size)]
        pltpu.make_async_copy(part, part, r3.at[g]).wait()
        zs[pl.ds(g, TOK, stride=8), :] = jnp.sum(part[...].astype(F32), axis=0)
    send4[...] = zs[...].reshape(NZ, BLOCK, LANES).astype(BF16)

    pltpu.make_async_copy(send4.at[0], recv4.at[0], r4).start()

    @pl.loop(1, NZ)
    def _(k):
        pltpu.make_async_remote_copy(
            send4.at[k], recv4.at[k], s4, r4,
            device_id=(2 * z_at(along(k)) + c, loc), device_id_type=MESH,
        ).start()

    pltpu.make_async_copy(pall, pall, rpa).wait()
    for g in range(GROUPS):
        at = 4 * (2 * (g % NX) + lax.rem(h + g // NX, 2))
        four = pall[at] + pall[at + 1] + pall[at + 2] + pall[at + 3]
        ptab[g : g + 1, :] = four[:1]
        ptab[GROUPS + g : GROUPS + g + 1, :] = four[1:]


    def prob_rows(home, names, first):
        sums = [jnp.zeros((8, LANES), F32) for _ in range(TOP)]
        groups = lax.broadcasted_iota(jnp.int32, (8, LANES), 0)
        for k in range(NZ):
            values = ptab[first : first + 8, :]
            hot = home[BLOCK * k : BLOCK * (k + 1), :].astype(F32).reshape(CAP, 8, LANES)
            found = jnp.zeros((8, LANES), F32)
            for r in range(CAP):
                found = found + hot[r] * values[:, CAP * k + r : CAP * k + r + 1]
            for kk in range(TOP):
                sums[kk] = sums[kk] + jnp.where(
                    names[kk : kk + 1, :] == groups + 8 * k, found, 0.0
                )
        return jnp.concatenate([jnp.sum(s, axis=0, keepdims=True) for s in sums], axis=0)

    sendx[FEAT:, :] = prob_rows(home_sib, rel1, 8)
    probs_mine = prob_rows(home_own, rel0, 0)

    pltpu.make_async_copy(recv4, recv4, r4).wait()
    back = recv4[...].reshape(NZ * BLOCK, LANES)
    sendx[:FEAT, :] = dot(back, home_sib[...], TN)[FEAT:]
    x_copy = pltpu.make_async_remote_copy(
        sendx, recvx, x_sem.at[0], x_sem.at[1], device_id=(sibling, loc), device_id_type=MESH
    )
    x_copy.start()
    mine = dot(back, home_own[...], TN)[:FEAT]
    x_copy.wait()
    small[:FEAT, :] = (mine + recvx[:FEAT, :])[:, :TOK]
    small[FEAT:, :] = (probs_mine + recvx[FEAT:, :])[:, :TOK] / prb[...].astype(F32)

    sent = recv1.at[pl.ds(0, 2 * NZ - 1)]
    pltpu.make_async_copy(sent, sent, s1).wait()
    for i in range(CHUNKS):
        sent = recv2.at[i, :, pl.ds(0, 3)]
        pltpu.make_async_copy(sent, sent, s2f.at[i]).wait()
        pltpu.make_async_copy(sent, sent, s2w.at[i]).wait()
        sent = recv2.at[i, 0, pl.ds(0, 7)]
        pltpu.make_async_copy(sent, sent, s2d.at[i]).wait()
    sent = recv3.at[pl.ds(0, 7)]
    pltpu.make_async_copy(sent, sent, s3d).wait()
    pltpu.make_async_copy(recvw, recvw, s3w).wait()
    pltpu.make_async_copy(sendf, sendf, s3f).wait()
    sent = pz.at[pl.ds(0, NZ - 1)]
    pltpu.make_async_copy(sent, sent, spz).wait()
    sent = pall.at[pl.ds(0, LOCAL - 1)]
    pltpu.make_async_copy(sent, sent, spa).wait()
    sent = recv4.at[pl.ds(0, NZ - 1)]
    pltpu.make_async_copy(sent, sent, s4).wait()
    gg_copy.wait()


def body(tokens, grad_out, probs, slot_of, w_gate, w_up, w_down):
    vmem, hbm = pl.BlockSpec(memory_space=pltpu.VMEM), pl.BlockSpec(memory_space=pl.ANY)
    dma = pltpu.SemaphoreType.DMA
    small, gate_grad = pl.pallas_call(
        kernel,
        out_shape=(
            jax.ShapeDtypeStruct((FEAT + TOP, TOK), F32),
            jax.ShapeDtypeStruct((1, QUARTER, WIDTH), BF16),
        ),
        in_specs=[vmem] * 4 + [hbm] * 3,
        out_specs=(vmem, hbm),
        scratch_shapes=[
            pltpu.VMEM((QUARTER, WIDTH), BF16),
            pltpu.VMEM((QUARTER, WIDTH), BF16),
            pltpu.VMEM((QUARTER, WIDTH), BF16),
            pltpu.VMEM((QUARTER, WIDTH), BF16),
            pltpu.VMEM((TOP, LANES), jnp.int32),
            pltpu.VMEM((TOP, LANES), jnp.int32),
            pltpu.VMEM((2 * FEAT, LANES), BF16),
            pltpu.VMEM((2 * FEAT, LANES), BF16),
            pltpu.VMEM((2 * NZ, BLOCK, LANES), BF16),
            pltpu.VMEM((2 * NZ, BLOCK, LANES), BF16),
            pltpu.VMEM((8 * BLOCK, LANES), F32),
            pltpu.VMEM((CHUNKS, GROUPS, BLOCK, LANES), BF16),
            pltpu.VMEM((CHUNKS, NX, NY, BLOCK, LANES), BF16),
            pltpu.VMEM((ROWS, WIDTH), BF16),
            pltpu.VMEM((ROWS, WIDTH), BF16),
            pltpu.VMEM((NX, NY, TOK, LANES), BF16),
            pltpu.VMEM((NX, 3, TOK, LANES), BF16),
            pltpu.VMEM((NX, 3, TOK, LANES), BF16),
            pltpu.VMEM((5 * NX, TOK, LANES), BF16),
            pltpu.VMEM((NZ * BLOCK, LANES), F32),
            pltpu.VMEM((NZ, BLOCK, LANES), BF16),
            pltpu.VMEM((NZ, BLOCK, LANES), BF16),
            pltpu.VMEM((FEAT + TOP, LANES), F32),
            pltpu.VMEM((FEAT + TOP, LANES), F32),
            pltpu.VMEM((NZ * BLOCK, LANES), BF16),
            pltpu.VMEM((NZ * BLOCK, LANES), BF16),
            pltpu.VMEM((2, LANES), F32),
            pltpu.VMEM((NZ, 2, LANES), F32),
            pltpu.VMEM((2, LANES), F32),
            pltpu.VMEM((LOCAL, 2, LANES), F32),
            pltpu.VMEM((2 * GROUPS, LANES), F32),
            dma((3,)),
            dma,
            dma((2,)),
            dma,
            dma((CHUNKS,)),
            dma((CHUNKS,)),
            dma((CHUNKS,)),
            dma((CHUNKS,)),
            dma((CHUNKS, NX)),
            dma((CHUNKS,)),
            dma((CHUNKS,)),
            dma,
            dma,
            dma,
            dma((NX,)),
            dma((GROUPS,)),
            dma,
            dma,
            dma((2,)),
            dma,
            dma,
            dma,
            dma,
        ],
        compiler_params=pltpu.CompilerParams(
            collective_id=0, has_side_effects=True, vmem_limit_bytes=60 * 1024 * 1024
        ),
    )(
        tokens.T, grad_out.T, probs.T, slot_of.T,
        jnp.swapaxes(w_gate, 1, 2), jnp.swapaxes(w_up, 1, 2), w_down,
    )
    return small[:FEAT].astype(BF16).T, small[FEAT:].T, jnp.swapaxes(gate_grad, 1, 2)


def solution(mesh):
    in_specs = (
        P("node", "local"),
        P("node", "local"),
        P("node", None),
        P("node", None),
        P(("node", "local"), None, None),
        P(("node", "local"), None, None),
        P(("node", "local"), None, None),
    )
    out_specs = (P("node", "local"), P("node", None), P(("node", "local"), None, None))
    return jax.shard_map(body, mesh=mesh, in_specs=in_specs, out_specs=out_specs, check_vma=False)
```
